128 devices in a mesh: dom: 8 (over z, core), tile: 16 (over y, x).
Axes of the slice: x: 4, y: 4, z: 4, core: 2. Of those that a mesh axis runs over, the one named last changes fastest.
Arguments:
- images: bfloat16 [512, 256, 256], P('dom', 'tile'), may hold values from -26 to 26
- defocus: float32 [512], P('dom'), may hold values from 0.5 to 3
- noise_weight: float32 [256, 128], P('tile'), may hold values from 0.5 to 4
- references: bfloat16 [2048, 256, 256], P(None, 'tile'), may hold values from -5 to 5
- candidates: int32 [512, 2], P('dom'), may hold values from 0 to 2047, as said below
- route: int32 [8, 16, 64, 2, 16], P('dom', 'tile'), may hold values from 0 to 127, as said below
- strips: int32 [8, 16, 64, 2, 16], P('dom', 'tile'), may hold values from 0 to 2047
Outputs:
- backprojection: float32 [262144, 384], P(('dom', 'tile'))
- spread: float32 [512], P('dom')
The draws below stay inside these ranges and needn't reach their ends.
Inputs may be any that keep to these rules, and one draw needn't show every extreme that they name: `candidates`: the 2 references of a particle differ. `route`: of the rows of one device, every owner receives either none or exactly 32; one owner, the same for all devices, receives 32 rows from every device.
All inputs are finite; a program needn't handle non-finite values.
Results may differ from the reference program's by a relative error of at most 0.005.
Values may be sent and summed in bfloat16 or wider, within the bound.
A program may use at most 128 MiB of HBM per device.

```python
import math
import jax
import jax.numpy as jnp
from jax import lax

HALF = 128
ROWS = 256
STRIPS = 2048
TOPK = 2
PD = 64
NREF = 2048
ROWS_DEV = 16
PARTICLES = 512
CAP = 32
TILES = 128
N_DOM = 8
N_TILE = 16
DEVICES = 128


def shared_refs(key):
    ref_key = jax.random.fold_in(key, 11)
    return jnp.clip(jax.random.normal(ref_key, (NREF, ROWS, 2 * HALF), jnp.float32), -5.0, 5.0)


def shared_cands(key):
    cand_key = jax.random.fold_in(key, 12)
    key_one, key_two = jax.random.split(cand_key)
    leading = jax.random.randint(key_one, (PARTICLES,), 0, NREF)
    leading = leading.at[0].set(NREF - 1)
    stride = jax.random.randint(key_two, (PARTICLES,), 1, NREF)
    return jnp.stack([leading, (leading + stride) % NREF], axis=1).astype(jnp.int32)


def shared_defocus(key):
    focus_key = jax.random.fold_in(key, 13)
    return jax.random.uniform(focus_key, (PARTICLES,), jnp.float32, 0.5, 3.0)


def draw_references(key, part):
    return shared_refs(key).astype(jnp.bfloat16)


def draw_candidates(key, part):
    return shared_cands(key)


def draw_defocus(key, part):
    return shared_defocus(key)


def draw_images(key, part):
    own_key = jax.random.fold_in(key, 21)
    key_four = jax.random.fold_in(own_key, 3)
    images = jnp.clip(jax.random.normal(key_four, (PARTICLES, ROWS, 2 * HALF), jnp.float32), -6.0, 6.0)
    return images.astype(jnp.bfloat16)


def draw_route(key, part):
    own_key = jax.random.fold_in(key, 31)
    hot_key, device_key = jax.random.split(own_key)
    hottest = jax.random.randint(hot_key, (), 0, DEVICES)
    row_total = PD * TOPK * ROWS_DEV

    def one_device(device):
        dev_key = jax.random.fold_in(device_key, device)
        key_one, key_two = jax.random.split(dev_key)
        others = (hottest + 1 + jax.random.permutation(key_one, DEVICES - 1)) % DEVICES
        owner_list = jnp.concatenate([hottest[None], others])
        slot_order = jax.random.permutation(key_two, row_total)
        return owner_list[slot_order // CAP]
    table = jax.vmap(one_device)(jnp.arange(DEVICES, dtype=jnp.int32))
    return table.reshape(N_DOM, N_TILE, PD, TOPK, ROWS_DEV).astype(jnp.int32)


def place_ends(values, key, smallest, top_value):
    longest = values.shape.index(max(values.shape))
    spots = []
    for shift in (0, 1):
        where = [jax.random.randint(jax.random.fold_in(key, axis), (), 0, length) for axis, length in enumerate(values.shape)]
        where[longest] = (where[longest] + shift) % values.shape[longest]
        spots.append(tuple(where))
    return values.at[spots[0]].set(smallest).at[spots[1]].set(top_value)


def block_levels(rng, extent, shards, smallest, largest):
    def one(dim, shards_of):
        heights = jax.random.uniform(jax.random.fold_in(jax.random.fold_in(rng, 6), dim), (shards_of,), jnp.float32, smallest / len(shards), largest / len(shards))
        return jnp.repeat(jnp.exp(heights), extent[dim] // shards_of).reshape((-1,) + (1,) * (len(extent) - dim - 1))

    loudness = one(*shards[0])
    for cut in shards[1:]:
        loudness = loudness * one(*cut)
    return loudness


def setup_inputs(seed: int = 0) -> dict:
    keys = jax.random.split(jax.random.key(seed), 8)
    return {
        "images": draw_images(jax.random.fold_in(keys[7], 71), 0),
        "defocus": draw_defocus(jax.random.fold_in(keys[7], 71), 0),
        "noise_weight": jnp.clip(jnp.exp(math.log(4.0) - 2.0794415 * jax.random.uniform(keys[2], (ROWS, HALF), jnp.float32) ** block_levels(keys[2], (ROWS, HALF), ((0, 16),), -0.2, 0.2)), 0.5, 4.0),
        "references": draw_references(jax.random.fold_in(keys[7], 71), 0),
        "candidates": draw_candidates(jax.random.fold_in(keys[7], 71), 0),
        "route": draw_route(jax.random.fold_in(keys[7], 71), 0),
        "strips": place_ends(jax.random.randint(keys[6], (N_DOM, N_TILE, PD, TOPK, ROWS_DEV), 0, STRIPS), jax.random.fold_in(keys[6], 1), 0, STRIPS - 1).astype(jnp.int32),
    }


CONTRAST_SCALE = 400.0
PHASE_SHIFT = 0.1

def contrast_table(defocus, row_start, row_count, all_rows, half_width):
    row_ids = row_start + jnp.arange(row_count, dtype=jnp.int32)
    row_freq = jnp.where(row_ids < all_rows // 2, row_ids, row_ids - all_rows).astype(jnp.float32)
    col_freq = jnp.arange(half_width, dtype=jnp.int32).astype(jnp.float32)
    radius = (row_freq[:, None] * row_freq[:, None] + col_freq[None, :] * col_freq[None, :]) / float(all_rows * all_rows)
    return -jnp.sin(CONTRAST_SCALE * defocus[:, None, None] * radius[None] + PHASE_SHIFT)

def reference(images, defocus, noise_weight, references, candidates, route, strips):
    contrast = contrast_table(defocus, 0, ROWS, ROWS, HALF)
    contrast_pair = jnp.concatenate([contrast, contrast], axis=2)
    weight_pair = jnp.concatenate([noise_weight, noise_weight], axis=1)
    weighted = (contrast_pair * weight_pair[None] * images.astype(jnp.float32)).astype(jnp.bfloat16)
    power_map = (contrast * contrast * noise_weight[None]).astype(jnp.bfloat16)
    ref_values = references.astype(jnp.float32)
    squares = (ref_values[:, :, :HALF] * ref_values[:, :, :HALF] + ref_values[:, :, HALF:] * ref_values[:, :, HALF:]).astype(jnp.bfloat16)
    contract_dims = (((1,), (1,)), ((), ()))
    crossed = lax.dot_general(weighted.reshape(PARTICLES, -1), references.reshape(NREF, -1), contract_dims, preferred_element_type=jnp.float32)
    energy = lax.dot_general(power_map.reshape(PARTICLES, -1), squares.reshape(NREF, -1), contract_dims, preferred_element_type=jnp.float32)
    scores = (crossed - 0.5 * energy) * (1.0 / math.sqrt(ROWS * HALF))
    highest = lax.optimization_barrier(jnp.max(scores, axis=1, keepdims=True))
    spread = jnp.log(lax.optimization_barrier(jnp.sum(jnp.exp(scores - highest), axis=1)))
    picked = jnp.take_along_axis(scores, candidates, axis=1)
    best_pick = lax.optimization_barrier(jnp.max(picked, axis=1, keepdims=True))
    raised = jnp.exp(picked - best_pick)
    chosen = raised / lax.optimization_barrier(jnp.sum(raised, axis=1, keepdims=True))
    weighted_kept, power_kept = lax.optimization_barrier((weighted, power_map))
    joined = jnp.concatenate([weighted_kept, power_kept], axis=2).astype(jnp.float32)
    owners = jnp.transpose(route, (0, 2, 3, 1, 4)).reshape(PARTICLES, TOPK, ROWS)
    strip_ids = jnp.transpose(strips, (0, 2, 3, 1, 4)).reshape(PARTICLES, TOPK, ROWS)
    target = owners * STRIPS + strip_ids
    volume = jnp.zeros((TILES * STRIPS, 3 * HALF), jnp.float32)
    for cand_idx in range(TOPK):
        rows_out = (chosen[:, cand_idx, None, None] * joined).astype(jnp.bfloat16)
        rows_out = lax.optimization_barrier(rows_out)
        volume = volume.at[target[:, cand_idx].reshape(-1)].add(rows_out.reshape(-1, 3 * HALF).astype(jnp.float32))
    return (volume, spread)
```

```python
import math

import jax
import jax.numpy as jnp
from jax import lax
from jax.experimental import pallas as pl
from jax.experimental.pallas import tpu as pltpu
from jax.sharding import PartitionSpec as P

F32 = jnp.float32
BF16 = jnp.bfloat16
I32 = jnp.int32
MESH = pl.DeviceIdType.MESH
NT = (((1,), (1,)), ((), ()))

STRIPS = 2048
HALF = 128
ROWS_DEV = 16
PD = 64
MINE = PD * ROWS_DEV
NREF = 2048
REFS = NREF // 2
WIDE = 3 * HALF
DEPTH = ROWS_DEV * WIDE
CHUNK = 256

TURN = 400.0 / 65536.0 / (2.0 * math.pi)
PHASE = 0.1 / (2.0 * math.pi)
SCALE = 1.0 / math.sqrt(32768.0)
SERIES = (
    6.283182793407029,
    -41.34141938561706,
    81.59613875538182,
    -76.5796878510169,
    41.20374363365668,
    -12.268859941003917,
)


def wave(turns):
    frac = turns - jnp.floor(turns + 0.5)
    sq = frac * frac
    total = jnp.full_like(sq, SERIES[-1])
    for coef in SERIES[-2::-1]:
        total = total * sq + coef
    return total * frac


def iota(shape, dim):
    return lax.broadcasted_iota(I32, shape, dim)


def kernel(
    img_ref, focus_ref, info_ref, noise_ref, refs_ref, owner_ref, strip_ref,
    vol_ref, spread_ref,
    rv, xc, xw, wi, pmo, ot, rank_ref, mask_ref, sb, rb, meta0, meta1, meta2,
    info, noise, score, part, stats, picks, stack, table, low, high, code, weight, pm,
    ref_sem, data_send, data_recv, xw_sem, info_sem, noise_sem, m1_sem, m2_sem, part_sem, stat_sem, pick_sem,
):
    dom = lax.axis_index("dom")
    tile = lax.axis_index("tile")
    core = lax.rem(dom, 2)
    barrier = pltpu.get_barrier_semaphore()

    def loads(c):
        return pltpu.make_async_copy(
            refs_ref.at[pl.ds(core * REFS + c * CHUNK, CHUNK)],
            rv.at[pl.ds(c * CHUNK, CHUNK)],
            ref_sem.at[c],
        )

    for c in range(REFS // CHUNK):
        loads(c).start()

    def greet(s, carry):
        pl.semaphore_signal(
            barrier,
            inc=1,
            device_id=(jnp.bitwise_xor(dom, s // 16), jnp.bitwise_xor(tile, lax.rem(s, 16))),
            device_id_type=MESH,
        )
        return carry

    lax.fori_loop(1, 128, greet, 0)

    def remote(src, dst, sems, d, t):
        return pltpu.make_async_remote_copy(
            src_ref=src, dst_ref=dst, send_sem=sems[0], recv_sem=sems[1],
            device_id=(d, t), device_id_type=MESH,
        )

    def pair(sem):
        return sem.at[0], sem.at[1]

    def wait_for(ref, sem):
        pltpu.make_async_copy(ref, ref, sem).wait()

    def freq_sq(rows):
        return jnp.where(rows < 128, rows, rows - 256).astype(F32)

    def weigh(c, carry):
        row_f = freq_sq(tile * 16 + iota((8, 16, HALF), 1))
        col_f = iota((8, 16, HALF), 2).astype(F32)
        radius = row_f * row_f + col_f * col_f
        focus = focus_ref[pl.ds(c * 8, 8)]
        contrast = -wave(focus * TURN * radius + PHASE)
        noise_here = noise_ref[...][None]
        power = (contrast * contrast * noise_here).astype(BF16)
        gain = contrast * noise_here
        start = pl.multiple_of(c * 128, 128)
        pmo[pl.ds(start, 128), :] = power.reshape(128, HALF)
        rows = img_ref[pl.ds(start, 128), :].astype(F32)
        gain = gain.reshape(128, HALF)
        wi[pl.ds(start, 128), 0:HALF] = (gain * rows[:, :HALF]).astype(BF16)
        wi[pl.ds(start, 128), HALF:] = (gain * rows[:, HALF:]).astype(BF16)
        return carry

    lax.fori_loop(0, 8, weigh, 0)

    ia, ib = iota((256, 256), 0), iota((256, 256), 1)
    swap = jnp.where(((ia & 15) * 16 + (ia >> 4)) == ib, 1.0, 0.0).astype(BF16)
    for b in range(4):
        at = pl.multiple_of(core * PD + b * 16, 16)
        left = jnp.dot(swap, wi[b * 256:(b + 1) * 256, :], preferred_element_type=F32).astype(BF16)
        right = (-0.5 * jnp.dot(swap, pmo[b * 256:(b + 1) * 256, :], preferred_element_type=F32)).astype(BF16)
        for i in range(16):
            xw[pl.ds(at, 16), i * WIDE:i * WIDE + 256] = left[i * 16:(i + 1) * 16]
            xw[pl.ds(at, 16), i * WIDE + 256:(i + 1) * WIDE] = right[i * 16:(i + 1) * 16]

    upper = jnp.where(ia < ib, 1.0, 0.0).astype(BF16)
    running = jnp.zeros((128, 1), F32)
    meta_low = jnp.zeros((128, 128), F32)
    meta_high = jnp.zeros((128, 128), F32)
    owner_id = iota((128, 256), 0)
    for k in range(2):
        for b in range(4):
            cols = slice(b * 256, (b + 1) * 256)
            owner = owner_ref[k:k + 1, cols]
            owner = ((owner & 15) << 3) | (owner >> 4)
            hit = jnp.where(owner_id == owner, 1.0, 0.0)
            hit16 = hit.astype(BF16)
            before = jnp.dot(hit16, upper, preferred_element_type=F32) + running
            rank = jnp.sum(hit * before, axis=0, keepdims=True)
            running = running + jnp.sum(hit, axis=1, keepdims=True)
            for t in range(16):
                ot[k, t, :, cols] = hit[t * 8:(t + 1) * 8]
            rank_ref[k:k + 1, cols] = rank
            strip = strip_ref[k:k + 1, cols] + 1
            number = iota((1, 256), 1) + b * 256
            group = owner_id >> 5
            same = (owner_id & 31).astype(F32) == rank
            low_value = jnp.where(group < 2, strip & 255, number & 255).astype(F32)
            high_value = jnp.where(group < 2, strip >> 8, (number >> 8) + 4 * k).astype(F32)
            low16 = jnp.where(same, low_value, 0.0).astype(BF16)
            high16 = jnp.where(same, high_value, 0.0).astype(BF16)
            meta_low = meta_low + lax.dot_general(hit16, low16, NT, preferred_element_type=F32)
            meta_high = meta_high + lax.dot_general(hit16, high16, NT, preferred_element_type=F32)
    meta = meta_low + 256.0 * meta_high
    for t in range(16):
        for d in range(8):
            meta0[t, d] = meta[t * 8 + d:t * 8 + d + 1, :]
    slot_id = iota((32, MINE), 0).astype(F32)
    for k in range(2):
        mask_ref[k] = jnp.where(slot_id == rank_ref[k:k + 1, :], 1.0, 0.0).astype(BF16)

    pl.semaphore_wait(barrier, 127)
    mate = jnp.bitwise_xor(dom, 1)
    mine = pl.ds(pl.multiple_of(core * PD, PD), PD)
    other = pl.ds(pl.multiple_of((1 - core) * PD, PD), PD)
    remote(xw.at[mine], xw.at[mine], pair(xw_sem), mate, tile).start()
    meta1[0] = meta0[tile]
    info[0] = info_ref[...]
    noise[0] = noise_ref[...]

    def small(u, carry):
        t = jnp.bitwise_xor(tile, u)
        remote(meta0.at[t], meta1.at[u], pair(m1_sem), dom, t).start()
        remote(noise_ref, noise.at[u], pair(noise_sem), dom, t).start()
        return carry

    lax.fori_loop(1, 16, small, 0)

    def small_dom(e, carry):
        remote(info_ref, info.at[e], pair(info_sem), jnp.bitwise_xor(dom, e), tile).start()
        return carry

    lax.fori_loop(1, 8, small_dom, 0)

    def pack(u):
        t = jnp.bitwise_xor(tile, u)
        blocks = []
        for d in range(8):
            one = ot[0, t, d:d + 1, :].astype(BF16)
            two = ot[1, t, d:d + 1, :].astype(BF16)
            blocks.append(mask_ref[0] * one + mask_ref[1] * two)
        rows = jnp.dot(jnp.concatenate(blocks, axis=0), wi[...], preferred_element_type=F32).astype(BF16)
        for d in range(8):
            sb[u, d] = rows[d * 32:(d + 1) * 32]
        return t

    def ship(u, e, t):
        d = jnp.bitwise_xor(dom, e)
        remote(sb.at[u, d], rb.at[u, e], (data_send, data_recv.at[u]), d, t).start()

    def rows_of(i, carry):
        u = lax.rem(i * 7, 16)
        t = pack(u)
        for e in range(8):
            ship(u, e, t)
        return carry

    lax.fori_loop(1, 16, rows_of, 0)
    here = pack(0)
    for e in range(1, 8):
        ship(0, e, here)
    rb[0, 0] = sb[0, dom]

    wait_for(meta1.at[pl.ds(1, 15)], m1_sem.at[1])
    for u in range(16):
        meta2[0, u] = meta1[u, dom]

    def forward(e, carry):
        d = jnp.bitwise_xor(dom, e)
        remote(meta1.at[:, d], meta2.at[e], pair(m2_sem), d, tile).start()
        return carry

    lax.fori_loop(1, 8, forward, 0)

    wait_for(xw.at[other], xw_sem.at[1])
    row = tile // 4
    column = lax.rem(tile, 4)
    for c in range(REFS // CHUNK):
        loads(c).wait()

    def scored(i, carry):
        chunk = jnp.bitwise_xor(row, lax.rem(i + 1, 4))
        base = pl.multiple_of(chunk * CHUNK, CHUNK)

        def block(b, inner):
            refs = rv[pl.ds(base + b * 16, 16)].reshape(256, 256)
            turned = jnp.dot(swap, refs, preferred_element_type=F32)
            squares = (turned[:, :HALF] * turned[:, :HALF] + turned[:, HALF:] * turned[:, HALF:]).astype(BF16)
            turned = turned.astype(BF16)
            at = pl.multiple_of(b * 16, 16)
            for r in range(16):
                xc[pl.ds(at, 16), r * WIDE:r * WIDE + 256] = turned[r * 16:(r + 1) * 16]
                xc[pl.ds(at, 16), r * WIDE + 256:(r + 1) * WIDE] = squares[r * 16:(r + 1) * 16]
            return inner

        lax.fori_loop(0, CHUNK // 16, block, 0)
        score[pl.ds(base, CHUNK), :] = SCALE * lax.dot_general(xc[...], xw[...], NT, preferred_element_type=F32)

        def share(v, inner):
            t = chunk * 4 + jnp.bitwise_xor(column, v)
            u = jnp.bitwise_xor(t, tile)

            @pl.when(u != 0)
            def _():
                remote(score.at[pl.ds(pl.multiple_of(t * 64, 64), 64)], part.at[u], pair(part_sem), dom, t).start()

            return inner

        lax.fori_loop(0, 4, share, 0)
        return carry

    lax.fori_loop(0, 4, scored, 0)
    part[0] = score[pl.ds(pl.multiple_of(tile * 64, 64), 64), :]

    wait_for(info.at[pl.ds(1, 7)], info_sem.at[1])
    wait_for(noise.at[pl.ds(1, 15)], noise_sem.at[1])
    wait_for(meta2.at[pl.ds(1, 7)], m2_sem.at[1])
    lane1 = iota((1, HALF), 1)
    stack[...] = jnp.zeros_like(stack)
    for w in range(4):
        focus = jnp.where(lane1 < PD, info[2 * w, 2:3, :], info[2 * w + 1, 2:3, :])
        first = focus.astype(BF16).astype(F32)
        second = (focus - first).astype(BF16).astype(F32)
        stack[4 * w:4 * w + 1, :] = first
        stack[4 * w + 1:4 * w + 2, :] = second
        stack[4 * w + 2:4 * w + 3, :] = focus - first - second
    focus_rows = stack[...].astype(BF16)
    lane2 = iota((1, 256), 1)

    def prepare(u, carry):
        quarter = lane1 >> 5
        strips, numbers = [], []
        for half in range(2):
            strip = jnp.zeros((1, HALF), F32)
            number = jnp.zeros((1, HALF), F32)
            for a in range(4):
                got = meta2[half * 4 + a, u]
                back = pltpu.roll(got, 64, 1)
                strip = jnp.where(quarter == a, got if a < 2 else back, strip)
                number = jnp.where(quarter == a, back if a < 2 else got, number)
            strips.append(strip)
            numbers.append(number)
        strip = jnp.concatenate(strips, axis=1).astype(I32) - 1
        number = jnp.concatenate(numbers, axis=1).astype(I32)
        low[u] = (strip & 255).astype(F32)
        high[u] = (strip >> 8).astype(F32)
        r = number & 15
        particle = ((number >> 4) & 63) + 64 * ((lane2 >> 5) & 1)
        code[u] = (particle + 128 * (number >> 10)).astype(F32)
        hot = jnp.where(iota((HALF, 256), 0) == particle, 1.0, 0.0).astype(BF16)
        found = jnp.dot(focus_rows, hot, preferred_element_type=F32)
        found = jnp.where((iota((16, 256), 0) >> 2) == (lane2 >> 6), found, 0.0)
        slope = jnp.sum(found, axis=0, keepdims=True) * TURN
        row_f = freq_sq(jnp.bitwise_xor(tile, u) * 16 + r)
        offset = slope * (row_f * row_f) + PHASE
        which = iota((8, 256), 0)
        rows = jnp.where(which == 0, slope, jnp.where(which == 1, offset, r.astype(F32)))
        turned = jnp.transpose(rows)
        col_f = iota((256, HALF), 1).astype(F32)
        contrast = wave(turned[:, 0:1] * (col_f * col_f) + turned[:, 1:2])
        pick_row = jnp.where((iota((256, 48), 1) & 15).astype(F32) == turned[:, 2:3], 1.0, 0.0).astype(BF16)
        full = noise[u]
        first = full.astype(BF16)
        second = (full - first.astype(F32)).astype(BF16)
        third = (full - first.astype(F32) - second.astype(F32)).astype(BF16)
        gain = jnp.dot(pick_row, jnp.concatenate([first, second, third], axis=0), preferred_element_type=F32)
        pm[u] = (contrast * contrast * gain).astype(BF16)
        return carry

    lax.fori_loop(0, 8, prepare, 0)

    wait_for(part.at[pl.ds(1, 15)], part_sem.at[1])
    total = part[0]
    for u in range(1, 16):
        total = total + part[u]
    same_core = jnp.where(core == 0, 0, 1)
    cand = []
    for k in range(2):
        zero = info[same_core, k:k + 1, :]
        one = info[1 - same_core, k:k + 1, :]
        cand.append(jnp.where(lane1 < PD, zero, one))
    ids = (iota((64, HALF), 0) + core * REFS + tile * 64).astype(F32)
    top = jnp.max(total, axis=0, keepdims=True)
    mass = jnp.sum(jnp.exp(total - top), axis=0, keepdims=True)
    got0 = jnp.sum(jnp.where(ids == cand[0], total, 0.0), axis=0, keepdims=True)
    got1 = jnp.sum(jnp.where(ids == cand[1], total, 0.0), axis=0, keepdims=True)
    which = iota((8, HALF), 0)
    stats[0] = jnp.where(which == 0, top, jnp.where(which == 1, mass, jnp.where(which == 2, got0, got1)))

    def tell(v, carry):
        d = jnp.bitwise_xor(dom, v // 16)
        t = jnp.bitwise_xor(tile, lax.rem(v, 16))
        remote(stats.at[0], stats.at[v], pair(stat_sem), d, t).start()
        return carry

    lax.fori_loop(1, 32, tell, 0)
    lax.fori_loop(8, 12, prepare, 0)
    wait_for(stats.at[pl.ds(1, 31)], stat_sem.at[1])
    every = stats[...]
    tops = every[:, 0, :]
    top = jnp.max(tops, axis=0, keepdims=True)
    mass = jnp.sum(every[:, 1, :] * jnp.exp(tops - top), axis=0, keepdims=True)
    got0 = jnp.sum(every[:, 2, :], axis=0, keepdims=True)
    got1 = jnp.sum(every[:, 3, :], axis=0, keepdims=True)
    spread = jnp.log(mass)
    best = jnp.maximum(got0, got1)
    raised0 = jnp.exp(got0 - best)
    raised1 = jnp.exp(got1 - best)
    chosen0 = raised0 / (raised0 + raised1)
    chosen1 = raised1 / (raised0 + raised1)
    rows = jnp.where(which == 0, chosen0, jnp.where(which == 1, chosen1, spread))
    rows = jnp.where(core == 0, rows, pltpu.roll(rows, 64, 1))
    picks[0] = rows
    spread_ref[...] = rows

    def pass_on(w, carry):
        remote(picks.at[0], picks.at[w], pair(pick_sem), jnp.bitwise_xor(dom, 2 * w), tile).start()
        return carry

    lax.fori_loop(1, 4, pass_on, 0)
    lax.fori_loop(12, 16, prepare, 0)
    wait_for(picks.at[pl.ds(1, 3)], pick_sem.at[1])
    for w in range(4):
        table[2 * w:2 * w + 2, :] = picks[w, 0:2, :]
    chosen_rows = table[...].astype(BF16)

    def choose(u, carry):
        number = code[u].astype(I32)
        hot = jnp.where(iota((HALF, 256), 0) == (number & 127), 1.0, 0.0).astype(BF16)
        found = jnp.dot(chosen_rows, hot, preferred_element_type=F32)
        keep = iota((8, 256), 0) == ((lane2 >> 6) * 2 + (number >> 7))
        weight[u] = jnp.sum(jnp.where(keep, found, 0.0), axis=0, keepdims=True)
        return carry

    lax.fori_loop(0, 16, choose, 0)

    order = [(i * 7) % 16 for i in range(1, 16)]
    del order
    slab_row = iota((256, 4 * 256), 0).astype(F32).astype(BF16)
    for g in range(4):
        for u in range(4 * g, 4 * g + 4):
            if u == 0:
                wait_for(rb.at[0, pl.ds(0, 7)], data_recv.at[0])
            else:
                wait_for(rb.at[u], data_recv.at[u])
        low16 = jnp.concatenate([low[u] for u in range(4 * g, 4 * g + 4)], axis=1).astype(BF16)
        high_row = jnp.concatenate([high[u] for u in range(4 * g, 4 * g + 4)], axis=1)
        share_row = jnp.concatenate([weight[u] for u in range(4 * g, 4 * g + 4)], axis=1)

        def insert(b, carry):
            value = jnp.where(high_row == b.astype(F32), share_row, 0.0).astype(BF16)
            spot = jnp.where(slab_row == low16, value, jnp.zeros_like(value))
            rows = rb[4 * g:4 * g + 4].reshape(1024, 256)
            power = pm[4 * g:4 * g + 4].reshape(1024, HALF)
            at = pl.ds(pl.multiple_of(b * 256, 256), 256)
            data = jnp.dot(spot, rows, preferred_element_type=F32)
            more = jnp.dot(spot, power, preferred_element_type=F32)
            if g == 0:
                vol_ref[at, 0:256] = data
                vol_ref[at, 256:] = more
            else:
                vol_ref[at, 0:256] += data
                vol_ref[at, 256:] += more
            return carry

        lax.fori_loop(0, 8, insert, 0)

    wait_for(xw.at[mine], xw_sem.at[0])
    wait_for(meta1.at[pl.ds(1, 15)], m1_sem.at[0])
    wait_for(noise.at[pl.ds(1, 15)], noise_sem.at[0])
    wait_for(info.at[pl.ds(1, 7)], info_sem.at[0])
    wait_for(meta2.at[pl.ds(1, 7)], m2_sem.at[0])
    wait_for(part.at[pl.ds(1, 15)], part_sem.at[0])
    wait_for(stats.at[pl.ds(1, 31)], stat_sem.at[0])
    wait_for(picks.at[pl.ds(1, 3)], pick_sem.at[0])
    wait_for(sb.at[pl.ds(1, 15)], data_send)
    wait_for(sb.at[0, pl.ds(0, 7)], data_send)


def shards(images, defocus, noise_weight, references, candidates, route, strips):
    rows = images.reshape(MINE, 2 * HALF)
    focus = jnp.broadcast_to(defocus[:, None, None], (PD, 1, HALF))
    cand = jnp.transpose(candidates).astype(F32)
    short = jnp.concatenate([cand, defocus[None], jnp.zeros((5, PD), F32)], axis=0)
    info = jnp.concatenate([short, short], axis=1)
    owners = jnp.transpose(route[0, 0], (1, 0, 2)).reshape(2, MINE)
    places = jnp.transpose(strips[0, 0], (1, 0, 2)).reshape(2, MINE)
    vmem = pl.BlockSpec(memory_space=pltpu.VMEM)
    dma = pltpu.SemaphoreType.DMA
    volume, spread = pl.pallas_call(
        kernel,
        out_shape=(
            jax.ShapeDtypeStruct((STRIPS, WIDE), F32),
            jax.ShapeDtypeStruct((8, HALF), F32),
        ),
        in_specs=[vmem, vmem, vmem, vmem, pl.BlockSpec(memory_space=pl.ANY), vmem, vmem],
        out_specs=(vmem, vmem),
        scratch_shapes=[
            pltpu.VMEM((REFS, ROWS_DEV, 2 * HALF), BF16),
            pltpu.VMEM((CHUNK, DEPTH), BF16),
            pltpu.VMEM((2 * PD, DEPTH), BF16),
            pltpu.VMEM((MINE, 2 * HALF), BF16),
            pltpu.VMEM((MINE, HALF), BF16),
            pltpu.VMEM((2, 16, 8, MINE), F32),
            pltpu.VMEM((2, MINE), F32),
            pltpu.VMEM((2, 32, MINE), BF16),
            pltpu.VMEM((16, 8, 32, 256), BF16),
            pltpu.VMEM((16, 8, 32, 256), BF16),
            pltpu.VMEM((16, 8, 1, HALF), F32),
            pltpu.VMEM((16, 8, 1, HALF), F32),
            pltpu.VMEM((8, 16, 1, HALF), F32),
            pltpu.VMEM((8, 8, HALF), F32),
            pltpu.VMEM((16, 16, HALF), F32),
            pltpu.VMEM((REFS, 2 * PD), F32),
            pltpu.VMEM((16, 64, 2 * PD), F32),
            pltpu.VMEM((32, 8, HALF), F32),
            pltpu.VMEM((4, 8, HALF), F32),
            pltpu.VMEM((16, HALF), F32),
            pltpu.VMEM((8, HALF), F32),
            pltpu.VMEM((16, 1, 256), F32),
            pltpu.VMEM((16, 1, 256), F32),
            pltpu.VMEM((16, 1, 256), F32),
            pltpu.VMEM((16, 1, 256), F32),
            pltpu.VMEM((16, 256, HALF), BF16),
            dma((REFS // CHUNK,)),
            dma,
            dma((16,)),
        ] + [dma((2,))] * 8,
        compiler_params=pltpu.CompilerParams(
            collective_id=0, has_side_effects=True, vmem_limit_bytes=56 << 20
        ),
    )(rows, focus, info, noise_weight, references, owners, places)
    return volume, spread[2, :PD]


def solution(mesh):
    in_specs = (
        P("dom", "tile", None),
        P("dom"),
        P("tile", None),
        P(None, "tile", None),
        P("dom", None),
        P("dom", "tile", None, None, None),
        P("dom", "tile", None, None, None),
    )
    out_specs = (P(("dom", "tile"), None), P("dom"))
    return jax.shard_map(shards, mesh=mesh, in_specs=in_specs, out_specs=out_specs, check_vma=False)
```

```python
import math

import jax
import jax.numpy as jnp
from jax import lax
from jax.experimental import pallas as pl
from jax.experimental.pallas import tpu as pltpu
from jax.sharding import PartitionSpec as P

F32 = jnp.float32
BF16 = jnp.bfloat16
I32 = jnp.int32
MESH = pl.DeviceIdType.MESH
NT = (((1,), (1,)), ((), ()))

STRIPS = 2048
HALF = 128
ROWS_DEV = 16
PD = 64
MINE = PD * ROWS_DEV
NREF = 2048
REFS = NREF // 2
WIDE = 3 * HALF
DEPTH = ROWS_DEV * WIDE
CHUNK = 256
EARLY = 8
FIRST, SECOND, THIRD = 8, 11, 14

TURN = 400.0 / 65536.0 / (2.0 * math.pi)
PHASE = 0.1 / (2.0 * math.pi)
SCALE = 1.0 / math.sqrt(32768.0)
SERIES = (
    6.283182793407029,
    -41.34141938561706,
    81.59613875538182,
    -76.5796878510169,
    41.20374363365668,
    -12.268859941003917,
)


def wave(turns):
    frac = turns - jnp.floor(turns + 0.5)
    sq = frac * frac
    total = jnp.full_like(sq, SERIES[-1])
    for coef in SERIES[-2::-1]:
        total = total * sq + coef
    return total * frac


def iota(shape, dim):
    return lax.broadcasted_iota(I32, shape, dim)


def kernel(
    img_ref, focus_ref, cand_ref, noise_ref, refs_ref, route_ref, place_ref,
    vol_ref, spread_ref,
    rv, xc, xw, wi, pmo, ot, rank_ref, mask_ref, sb, rb, meta0, meta1, meta2,
    lanes, info, noise, score, part, stats, picks, stack, table, low, high, code, weight, pm,
    ref_sem, data_send, data_recv, all_sem, xw_sem, info_sem, noise_sem, m1_sem, m2_sem, part_sem, stat_sem, pick_sem,
):
    dom = lax.axis_index("dom")
    tile = lax.axis_index("tile")
    core = lax.rem(dom, 2)
    barrier = pltpu.get_barrier_semaphore()

    def loads(c):
        return pltpu.make_async_copy(
            refs_ref.at[pl.ds(core * REFS + c * CHUNK, CHUNK)],
            rv.at[pl.ds(c * CHUNK, CHUNK)],
            ref_sem.at[c],
        )

    for c in range(REFS // CHUNK):
        loads(c).start()

    def greet_tile(u, carry):
        pl.semaphore_signal(barrier, inc=1, device_id=(dom, jnp.bitwise_xor(tile, u)), device_id_type=MESH)
        return carry

    def greet_dom(e, carry):
        pl.semaphore_signal(barrier, inc=1, device_id=(jnp.bitwise_xor(dom, e), tile), device_id_type=MESH)
        return carry

    def vouch(e, carry):
        pl.semaphore_signal(all_sem, inc=1, device_id=(jnp.bitwise_xor(dom, e), tile), device_id_type=MESH)
        return carry

    lax.fori_loop(1, 16, greet_tile, 0)
    lax.fori_loop(1, 8, greet_dom, 0)

    def remote(src, dst, sems, d, t):
        return pltpu.make_async_remote_copy(
            src_ref=src, dst_ref=dst, send_sem=sems[0], recv_sem=sems[1],
            device_id=(d, t), device_id_type=MESH,
        )

    def pair(sem):
        return sem.at[0], sem.at[1]

    def wait_for(ref, sem):
        pltpu.make_async_copy(ref, ref, sem).wait()

    info[0] = jnp.zeros((8, HALF), F32)
    for k in range(2):
        cand_row = cand_ref[k:k + 1, :].astype(F32)
        info[0, k:k + 1, :] = jnp.concatenate([cand_row, cand_row], axis=1)
    info[0, 2:3, :] = jnp.concatenate([focus_ref[...], focus_ref[...]], axis=1)
    widen = jnp.where((iota((PD, MINE), 1) >> 4) == iota((PD, MINE), 0), 1.0, 0.0).astype(BF16)
    diagonal = (iota((16, MINE), 1) & 15) == iota((16, MINE), 0)

    def along(block):
        wide = jnp.dot(block.astype(F32).astype(BF16), widen, preferred_element_type=F32)
        return jnp.sum(jnp.where(diagonal, wide, 0.0), axis=0, keepdims=True)

    for k in range(2):
        lanes[k:k + 1, :] = along(route_ref[k])
        place = place_ref[k] + 1
        lanes[2 + k:3 + k, :] = along(place & 255)
        lanes[4 + k:5 + k, :] = along(place >> 8)

    def freq_sq(rows):
        return jnp.where(rows < 128, rows, rows - 256).astype(F32)

    focus_row = info[0, 2:3, :]

    def weigh(c, carry):
        row = iota((128, HALF), 0)
        lane = iota((128, HALF), 1)
        row_f = freq_sq(tile * 16 + (row & 15))
        col_f = lane.astype(F32)
        radius = row_f * row_f + col_f * col_f
        focus = jnp.sum(jnp.where(lane == c * 8 + (row >> 4), focus_row, 0.0), axis=1, keepdims=True)
        contrast = -wave(focus * TURN * radius + PHASE)
        noise_here = jnp.concatenate([noise_ref[...]] * 8, axis=0)
        start = pl.multiple_of(c * 128, 128)
        pmo[pl.ds(start, 128), :] = (contrast * contrast * noise_here).astype(BF16)
        gain = contrast * noise_here
        rows = img_ref[pl.ds(start, 128), :].astype(F32)
        wi[pl.ds(start, 128), 0:HALF] = (gain * rows[:, :HALF]).astype(BF16)
        wi[pl.ds(start, 128), HALF:] = (gain * rows[:, HALF:]).astype(BF16)
        return carry

    lax.fori_loop(0, 8, weigh, 0)

    ia, ib = iota((256, 256), 0), iota((256, 256), 1)
    swap = jnp.where(((ia & 15) * 16 + (ia >> 4)) == ib, 1.0, 0.0).astype(BF16)
    for b in range(4):
        at = pl.multiple_of(core * PD + b * 16, 16)
        left = jnp.dot(swap, wi[b * 256:(b + 1) * 256, :], preferred_element_type=F32).astype(BF16)
        right = (-0.5 * jnp.dot(swap, pmo[b * 256:(b + 1) * 256, :], preferred_element_type=F32)).astype(BF16)
        for i in range(16):
            xw[pl.ds(at, 16), i * WIDE:i * WIDE + 256] = left[i * 16:(i + 1) * 16]
            xw[pl.ds(at, 16), i * WIDE + 256:(i + 1) * WIDE] = right[i * 16:(i + 1) * 16]

    upper = jnp.where(ia < ib, 1.0, 0.0).astype(BF16)
    running = jnp.zeros((128, 1), F32)
    meta_low = jnp.zeros((128, 128), F32)
    meta_high = jnp.zeros((128, 128), F32)
    owner_id = iota((128, 256), 0)
    for k in range(2):
        for b in range(4):
            cols = slice(b * 256, (b + 1) * 256)
            owner = lanes[k:k + 1, cols].astype(I32)
            owner = ((owner & 15) << 3) | (owner >> 4)
            hit = jnp.where(owner_id == owner, 1.0, 0.0)
            hit16 = hit.astype(BF16)
            before = jnp.dot(hit16, upper, preferred_element_type=F32) + running
            rank = jnp.sum(hit * before, axis=0, keepdims=True)
            running = running + jnp.sum(hit, axis=1, keepdims=True)
            for t in range(16):
                ot[k, t, :, cols] = hit[t * 8:(t + 1) * 8]
            rank_ref[k:k + 1, cols] = rank
            number = iota((1, 256), 1) + b * 256
            group = owner_id >> 5
            same = (owner_id & 31).astype(F32) == rank
            low_value = jnp.where(group < 2, lanes[2 + k:3 + k, cols], (number & 255).astype(F32))
            high_value = jnp.where(group < 2, lanes[4 + k:5 + k, cols], ((number >> 8) + 4 * k).astype(F32))
            low16 = jnp.where(same, low_value, 0.0).astype(BF16)
            high16 = jnp.where(same, high_value, 0.0).astype(BF16)
            meta_low = meta_low + lax.dot_general(hit16, low16, NT, preferred_element_type=F32)
            meta_high = meta_high + lax.dot_general(hit16, high16, NT, preferred_element_type=F32)
    meta = meta_low + 256.0 * meta_high
    for t in range(16):
        for d in range(8):
            meta0[t, d] = meta[t * 8 + d:t * 8 + d + 1, :]
    slot_id = iota((32, MINE), 0).astype(F32)
    for k in range(2):
        mask_ref[k] = jnp.where(slot_id == rank_ref[k:k + 1, :], 1.0, 0.0).astype(BF16)

    def turn_of(i):
        return lax.rem(7 * (i + 1), 16)

    def pack(i, carry):
        t = jnp.bitwise_xor(tile, turn_of(i))
        blocks = []
        for d in range(8):
            one = ot[0, t, d:d + 1, :].astype(BF16)
            two = ot[1, t, d:d + 1, :].astype(BF16)
            blocks.append(mask_ref[0] * one + mask_ref[1] * two)
        rows = jnp.dot(jnp.concatenate(blocks, axis=0), wi[...], preferred_element_type=F32).astype(BF16)
        for d in range(8):
            sb[i, d] = rows[d * 32:(d + 1) * 32]
        return carry

    lax.fori_loop(0, EARLY, pack, 0)

    pl.semaphore_wait(barrier, 22)
    lax.fori_loop(1, 8, vouch, 0)
    mate = jnp.bitwise_xor(dom, 1)
    mine = pl.ds(pl.multiple_of(core * PD, PD), PD)
    other = pl.ds(pl.multiple_of((1 - core) * PD, PD), PD)
    remote(xw.at[mine], xw.at[mine], pair(xw_sem), mate, tile).start()
    meta1[0] = meta0[tile]
    noise[0] = noise_ref[...]

    def small(u, carry):
        t = jnp.bitwise_xor(tile, u)
        remote(meta0.at[t], meta1.at[u], pair(m1_sem), dom, t).start()
        remote(noise_ref, noise.at[u], pair(noise_sem), dom, t).start()
        return carry

    lax.fori_loop(1, 16, small, 0)

    def small_dom(e, carry):
        remote(info.at[0], info.at[e], pair(info_sem), jnp.bitwise_xor(dom, e), tile).start()
        return carry

    lax.fori_loop(1, 8, small_dom, 0)

    pl.semaphore_wait(all_sem, 7)

    def ship(i, carry):
        t = jnp.bitwise_xor(tile, turn_of(i))
        for e in range(8):
            d = jnp.bitwise_xor(dom, e)
            remote(sb.at[i, d], rb.at[i, e], (data_send, data_recv.at[i]), d, t).start()
        return carry

    lax.fori_loop(0, FIRST, ship, 0)
    lax.fori_loop(EARLY, 16, pack, 0)
    rb[15, 0] = sb[15, dom]

    wait_for(meta1.at[pl.ds(1, 15)], m1_sem.at[1])
    for u in range(16):
        meta2[0, u] = meta1[u, dom]

    def forward(e, carry):
        d = jnp.bitwise_xor(dom, e)
        remote(meta1.at[:, d], meta2.at[e], pair(m2_sem), d, tile).start()
        return carry

    lax.fori_loop(1, 8, forward, 0)

    wait_for(xw.at[other], xw_sem.at[1])
    row = tile // 4
    column = lax.rem(tile, 4)
    for c in range(REFS // CHUNK):
        loads(c).wait()

    def scored(i, carry):
        chunk = jnp.bitwise_xor(row, lax.rem(i + 1, 4))
        base = pl.multiple_of(chunk * CHUNK, CHUNK)

        def block(b, inner):
            refs = rv[pl.ds(base + b * 16, 16)].reshape(256, 256)
            turned = jnp.dot(swap, refs, preferred_element_type=F32)
            squares = (turned[:, :HALF] * turned[:, :HALF] + turned[:, HALF:] * turned[:, HALF:]).astype(BF16)
            turned = turned.astype(BF16)
            at = pl.multiple_of(b * 16, 16)
            for r in range(16):
                xc[pl.ds(at, 16), r * WIDE:r * WIDE + 256] = turned[r * 16:(r + 1) * 16]
                xc[pl.ds(at, 16), r * WIDE + 256:(r + 1) * WIDE] = squares[r * 16:(r + 1) * 16]
            return inner

        lax.fori_loop(0, CHUNK // 16, block, 0, unroll=4)
        score[pl.ds(base, CHUNK), :] = SCALE * lax.dot_general(xc[...], xw[...], NT, preferred_element_type=F32)

        def share(v, inner):
            t = chunk * 4 + jnp.bitwise_xor(column, v)
            u = jnp.bitwise_xor(t, tile)

            @pl.when(u != 0)
            def _():
                remote(score.at[pl.ds(pl.multiple_of(t * 64, 64), 64)], part.at[u], pair(part_sem), dom, t).start()

            return inner

        lax.fori_loop(0, 4, share, 0)
        return carry

    lax.fori_loop(0, 4, scored, 0)
    part[0] = score[pl.ds(pl.multiple_of(tile * 64, 64), 64), :]
    lax.fori_loop(FIRST, SECOND, ship, 0)

    wait_for(info.at[pl.ds(1, 7)], info_sem.at[1])
    wait_for(noise.at[pl.ds(1, 15)], noise_sem.at[1])
    wait_for(meta2.at[pl.ds(1, 7)], m2_sem.at[1])
    lane1 = iota((1, HALF), 1)
    stack[...] = jnp.zeros_like(stack)
    for w in range(4):
        focus = jnp.where(lane1 < PD, info[2 * w, 2:3, :], info[2 * w + 1, 2:3, :])
        first = focus.astype(BF16).astype(F32)
        second = (focus - first).astype(BF16).astype(F32)
        stack[4 * w:4 * w + 1, :] = first
        stack[4 * w + 1:4 * w + 2, :] = second
        stack[4 * w + 2:4 * w + 3, :] = focus - first - second
    focus_rows = stack[...].astype(BF16)
    lane2 = iota((1, 256), 1)

    def prepare(i, carry):
        u = turn_of(i)
        quarter = lane1 >> 5
        strips, numbers = [], []
        for half in range(2):
            strip = jnp.zeros((1, HALF), F32)
            number = jnp.zeros((1, HALF), F32)
            for a in range(4):
                got = meta2[half * 4 + a, u]
                back = pltpu.roll(got, 64, 1)
                strip = jnp.where(quarter == a, got if a < 2 else back, strip)
                number = jnp.where(quarter == a, back if a < 2 else got, number)
            strips.append(strip)
            numbers.append(number)
        strip = jnp.concatenate(strips, axis=1).astype(I32) - 1
        number = jnp.concatenate(numbers, axis=1).astype(I32)
        low[i] = (strip & 255).astype(F32)
        high[i] = (strip >> 8).astype(F32)
        r = number & 15
        particle = ((number >> 4) & 63) + 64 * ((lane2 >> 5) & 1)
        code[i] = (particle + 128 * (number >> 10)).astype(F32)
        hot = jnp.where(iota((HALF, 256), 0) == particle, 1.0, 0.0).astype(BF16)
        found = jnp.dot(focus_rows, hot, preferred_element_type=F32)
        found = jnp.where((iota((16, 256), 0) >> 2) == (lane2 >> 6), found, 0.0)
        slope = jnp.sum(found, axis=0, keepdims=True) * TURN
        row_f = freq_sq(jnp.bitwise_xor(tile, u) * 16 + r)
        offset = slope * (row_f * row_f) + PHASE
        which = iota((8, 256), 0)
        rows = jnp.where(which == 0, slope, jnp.where(which == 1, offset, jnp.where(which == 2, r.astype(F32), strip.astype(F32))))
        turned = jnp.transpose(rows)
        col_f = iota((256, HALF), 1).astype(F32)
        contrast = wave(turned[:, 0:1] * (col_f * col_f) + turned[:, 1:2])
        pick_row = jnp.where((iota((256, 48), 1) & 15).astype(F32) == turned[:, 2:3], 1.0, 0.0).astype(BF16)
        full = noise[u]
        first = full.astype(BF16)
        second = (full - first.astype(F32)).astype(BF16)
        third = (full - first.astype(F32) - second.astype(F32)).astype(BF16)
        gain = jnp.dot(pick_row, jnp.concatenate([first, second, third], axis=0), preferred_element_type=F32)
        power = contrast * contrast * gain
        upper_half = turned[:, 3:4] >= 1024.0
        pm[i, :, 0:HALF] = jnp.where(upper_half, 0.0, power).astype(BF16)
        pm[i, :, HALF:] = jnp.where(upper_half, power, 0.0).astype(BF16)
        return carry

    lax.fori_loop(0, 8, prepare, 0)

    wait_for(part.at[pl.ds(1, 15)], part_sem.at[1])
    total = part[0]
    for u in range(1, 16):
        total = total + part[u]
    same_core = jnp.where(core == 0, 0, 1)
    cand = []
    for k in range(2):
        zero = info[same_core, k:k + 1, :]
        one = info[1 - same_core, k:k + 1, :]
        cand.append(jnp.where(lane1 < PD, zero, one))
    ids = (iota((64, HALF), 0) + core * REFS + tile * 64).astype(F32)
    top = jnp.max(total, axis=0, keepdims=True)
    mass = jnp.sum(jnp.exp(total - top), axis=0, keepdims=True)
    got0 = jnp.sum(jnp.where(ids == cand[0], total, 0.0), axis=0, keepdims=True)
    got1 = jnp.sum(jnp.where(ids == cand[1], total, 0.0), axis=0, keepdims=True)
    which = iota((8, HALF), 0)
    stats[0] = jnp.where(which == 0, top, jnp.where(which == 1, mass, jnp.where(which == 2, got0, got1)))

    def tell(v, carry):
        d = jnp.bitwise_xor(dom, v // 16)
        t = jnp.bitwise_xor(tile, lax.rem(v, 16))
        remote(stats.at[0], stats.at[v], pair(stat_sem), d, t).start()
        return carry

    lax.fori_loop(1, 32, tell, 0)
    lax.fori_loop(SECOND, THIRD, ship, 0)
    lax.fori_loop(8, 12, prepare, 0)
    wait_for(stats.at[pl.ds(1, 31)], stat_sem.at[1])
    every = stats[...]
    tops = every[:, 0, :]
    top = jnp.max(tops, axis=0, keepdims=True)
    mass = jnp.sum(every[:, 1, :] * jnp.exp(tops - top), axis=0, keepdims=True)
    got0 = jnp.sum(every[:, 2, :], axis=0, keepdims=True)
    got1 = jnp.sum(every[:, 3, :], axis=0, keepdims=True)
    spread = jnp.log(mass)
    best = jnp.maximum(got0, got1)
    raised0 = jnp.exp(got0 - best)
    raised1 = jnp.exp(got1 - best)
    chosen0 = raised0 / (raised0 + raised1)
    chosen1 = raised1 / (raised0 + raised1)
    rows = jnp.where(which == 0, chosen0, jnp.where(which == 1, chosen1, spread))
    rows = jnp.where(core == 0, rows, pltpu.roll(rows, 64, 1))
    picks[0] = rows
    spread_ref[...] = rows

    def pass_on(w, carry):
        remote(picks.at[0], picks.at[w], pair(pick_sem), jnp.bitwise_xor(dom, 2 * w), tile).start()
        return carry

    lax.fori_loop(1, 4, pass_on, 0)
    lax.fori_loop(THIRD, 15, ship, 0)

    def ship_last(e, carry):
        d = jnp.bitwise_xor(dom, e)
        remote(sb.at[15, d], rb.at[15, e], (data_send, data_recv.at[15]), d, tile).start()
        return carry

    lax.fori_loop(1, 8, ship_last, 0)
    lax.fori_loop(12, 16, prepare, 0)
    wait_for(picks.at[pl.ds(1, 3)], pick_sem.at[1])
    for w in range(4):
        table[2 * w:2 * w + 2, :] = picks[w, 0:2, :]
    chosen_rows = table[...].astype(BF16)

    def choose(u, carry):
        number = code[u].astype(I32)
        hot = jnp.where(iota((HALF, 256), 0) == (number & 127), 1.0, 0.0).astype(BF16)
        found = jnp.dot(chosen_rows, hot, preferred_element_type=F32)
        keep = iota((8, 256), 0) == ((lane2 >> 6) * 2 + (number >> 7))
        weight[u] = jnp.sum(jnp.where(keep, found, 0.0), axis=0, keepdims=True)
        return carry

    lax.fori_loop(0, 16, choose, 0)

    slab_row = iota((256, 4 * 256), 0).astype(F32).astype(BF16)
    for g in range(4):
        for i in range(4 * g, 4 * g + 4):
            if i == 15:
                wait_for(rb.at[15, pl.ds(1, 7)], data_recv.at[15])
            else:
                wait_for(rb.at[i], data_recv.at[i])
        low16 = jnp.concatenate([low[i] for i in range(4 * g, 4 * g + 4)], axis=1).astype(BF16)
        high_row = jnp.concatenate([high[i] for i in range(4 * g, 4 * g + 4)], axis=1)
        share_row = jnp.concatenate([weight[i] for i in range(4 * g, 4 * g + 4)], axis=1)

        def insert(b, carry):
            match = slab_row == low16
            rows = rb[4 * g:4 * g + 4].reshape(1024, 256)
            power = pm[4 * g:4 * g + 4].reshape(1024, 256)
            spots = []
            for h in range(2):
                value = jnp.where(high_row == (b + 4 * h).astype(F32), share_row, 0.0).astype(BF16)
                spots.append(jnp.where(match, value, jnp.zeros_like(value)))
            both = jnp.dot(spots[0] + spots[1], power, preferred_element_type=F32)
            for h in range(2):
                at = pl.ds(pl.multiple_of((b + 4 * h) * 256, 256), 256)
                data = jnp.dot(spots[h], rows, preferred_element_type=F32)
                more = both[:, h * HALF:(h + 1) * HALF]
                if g == 0:
                    vol_ref[at, 0:256] = data
                    vol_ref[at, 256:] = more
                else:
                    vol_ref[at, 0:256] += data
                    vol_ref[at, 256:] += more
            return carry

        lax.fori_loop(0, 4, insert, 0)

    wait_for(xw.at[mine], xw_sem.at[0])
    wait_for(meta1.at[pl.ds(1, 15)], m1_sem.at[0])
    wait_for(noise.at[pl.ds(1, 15)], noise_sem.at[0])
    wait_for(info.at[pl.ds(1, 7)], info_sem.at[0])
    wait_for(meta2.at[pl.ds(1, 7)], m2_sem.at[0])
    wait_for(part.at[pl.ds(1, 15)], part_sem.at[0])
    wait_for(stats.at[pl.ds(1, 31)], stat_sem.at[0])
    wait_for(picks.at[pl.ds(1, 3)], pick_sem.at[0])
    wait_for(sb.at[pl.ds(0, 15)], data_send)
    wait_for(sb.at[15, pl.ds(0, 7)], data_send)


def shards(images, defocus, noise_weight, references, candidates, route, strips):
    rows = images.reshape(MINE, 2 * HALF)
    focus = defocus[None]
    turned = [jnp.transpose(x[0, 0], (1, 2, 0)) for x in (route, strips)]
    vmem = pl.BlockSpec(memory_space=pltpu.VMEM)
    dma = pltpu.SemaphoreType.DMA
    volume, spread = pl.pallas_call(
        kernel,
        out_shape=(
            jax.ShapeDtypeStruct((STRIPS, WIDE), F32),
            jax.ShapeDtypeStruct((8, HALF), F32),
        ),
        in_specs=[vmem, vmem, vmem, vmem, pl.BlockSpec(memory_space=pl.ANY), vmem, vmem],
        out_specs=(vmem, vmem),
        scratch_shapes=[
            pltpu.VMEM((REFS, ROWS_DEV, 2 * HALF), BF16),
            pltpu.VMEM((CHUNK, DEPTH), BF16),
            pltpu.VMEM((2 * PD, DEPTH), BF16),
            pltpu.VMEM((MINE, 2 * HALF), BF16),
            pltpu.VMEM((MINE, HALF), BF16),
            pltpu.VMEM((2, 16, 8, MINE), F32),
            pltpu.VMEM((2, MINE), F32),
            pltpu.VMEM((2, 32, MINE), BF16),
            pltpu.VMEM((16, 8, 32, 256), BF16),
            pltpu.VMEM((16, 8, 32, 256), BF16),
            pltpu.VMEM((16, 8, 1, HALF), F32),
            pltpu.VMEM((16, 8, 1, HALF), F32),
            pltpu.VMEM((8, 16, 1, HALF), F32),
            pltpu.VMEM((8, MINE), F32),
            pltpu.VMEM((8, 8, HALF), F32),
            pltpu.VMEM((16, 16, HALF), F32),
            pltpu.VMEM((REFS, 2 * PD), F32),
            pltpu.VMEM((16, 64, 2 * PD), F32),
            pltpu.VMEM((32, 8, HALF), F32),
            pltpu.VMEM((4, 8, HALF), F32),
            pltpu.VMEM((16, HALF), F32),
            pltpu.VMEM((8, HALF), F32),
            pltpu.VMEM((16, 1, 256), F32),
            pltpu.VMEM((16, 1, 256), F32),
            pltpu.VMEM((16, 1, 256), F32),
            pltpu.VMEM((16, 1, 256), F32),
            pltpu.VMEM((16, 256, 256), BF16),
            dma((REFS // CHUNK,)),
            dma,
            dma((16,)),
            pltpu.SemaphoreType.REGULAR,
        ] + [dma((2,))] * 8,
        compiler_params=pltpu.CompilerParams(
            collective_id=0, has_side_effects=True, vmem_limit_bytes=56 << 20
        ),
    )(rows, focus, candidates.T, noise_weight, references, *turned)
    return volume, spread[2, :PD]


def solution(mesh):
    in_specs = (
        P("dom", "tile", None),
        P("dom"),
        P("tile", None),
        P(None, "tile", None),
        P("dom", None),
        P("dom", "tile", None, None, None),
        P("dom", "tile", None, None, None),
    )
    out_specs = (P(("dom", "tile"), None), P("dom"))
    return jax.shard_map(shards, mesh=mesh, in_specs=in_specs, out_specs=out_specs, check_vma=False)
```

```python
import math

import jax
import jax.numpy as jnp
from jax import lax
from jax.experimental import pallas as pl
from jax.experimental.pallas import tpu as pltpu
from jax.sharding import PartitionSpec as P

F32 = jnp.float32
BF16 = jnp.bfloat16
I32 = jnp.int32
MESH = pl.DeviceIdType.MESH
NT = (((1,), (1,)), ((), ()))

STRIPS = 2048
HALF = 128
ROWS_DEV = 16
PD = 64
MINE = PD * ROWS_DEV
NREF = 2048
REFS = NREF // 2
WIDE = 3 * HALF
DEPTH = ROWS_DEV * WIDE
CHUNK = 256
FIRST, SECOND, THIRD = 6, 8, 11
SHIFT = (0, 5, 10, 15, 3, 6, 9, 12)

TURN = 400.0 / 65536.0 / (2.0 * math.pi)
PHASE = 0.1 / (2.0 * math.pi)
SCALE = 1.0 / math.sqrt(32768.0)
SERIES = (
    6.283182793407029,
    -41.34141938561706,
    81.59613875538182,
    -76.5796878510169,
    41.20374363365668,
    -12.268859941003917,
)


def wave(turns):
    frac = turns - jnp.floor(turns + 0.5)
    sq = frac * frac
    total = jnp.full_like(sq, SERIES[-1])
    for coef in SERIES[-2::-1]:
        total = total * sq + coef
    return total * frac


def iota(shape, dim):
    return lax.broadcasted_iota(I32, shape, dim)


def kernel(
    img_ref, focus_ref, cand_ref, noise_ref, refs_ref, route_ref, place_ref,
    vol_ref, spread_ref,
    rv, xc, xw, wi, pmo, ot, rank_ref, mask_ref, sb, rb, meta0, meta1, meta2,
    lanes, info, noise, score, part, stats, picks, stack, table, low, high, code, weight, pm,
    ref_sem, data_send, data_recv, all_sem, xw_sem, info_sem, noise_sem, m1_sem, m2_sem, part_sem, stat_sem, pick_sem,
):
    dom = lax.axis_index("dom")
    tile = lax.axis_index("tile")
    core = lax.rem(dom, 2)
    barrier = pltpu.get_barrier_semaphore()

    def loads(c):
        return pltpu.make_async_copy(
            refs_ref.at[pl.ds(core * REFS + c * CHUNK, CHUNK)],
            rv.at[pl.ds(c * CHUNK, CHUNK)],
            ref_sem.at[c],
        )

    for c in range(REFS // CHUNK):
        loads(c).start()

    def greet_tile(u, carry):
        pl.semaphore_signal(barrier, inc=1, device_id=(dom, jnp.bitwise_xor(tile, u)), device_id_type=MESH)
        return carry

    def greet_dom(e, carry):
        pl.semaphore_signal(barrier, inc=1, device_id=(jnp.bitwise_xor(dom, e), tile), device_id_type=MESH)
        return carry

    def vouch(e, carry):
        pl.semaphore_signal(all_sem, inc=1, device_id=(jnp.bitwise_xor(dom, e), tile), device_id_type=MESH)
        return carry

    lax.fori_loop(1, 16, greet_tile, 0)
    lax.fori_loop(1, 8, greet_dom, 0)

    def remote(src, dst, sems, d, t):
        return pltpu.make_async_remote_copy(
            src_ref=src, dst_ref=dst, send_sem=sems[0], recv_sem=sems[1],
            device_id=(d, t), device_id_type=MESH,
        )

    def pair(sem):
        return sem.at[0], sem.at[1]

    def wait_for(ref, sem):
        pltpu.make_async_copy(ref, ref, sem).wait()

    info[0] = jnp.zeros((8, HALF), F32)
    for k in range(2):
        cand_row = cand_ref[k:k + 1, :].astype(F32)
        info[0, k:k + 1, :] = jnp.concatenate([cand_row, cand_row], axis=1)
    info[0, 2:3, :] = jnp.concatenate([focus_ref[...], focus_ref[...]], axis=1)
    widen = jnp.where((iota((PD, MINE), 1) >> 4) == iota((PD, MINE), 0), 1.0, 0.0).astype(BF16)
    diagonal = (iota((16, MINE), 1) & 15) == iota((16, MINE), 0)

    def along(block):
        wide = jnp.dot(block.astype(F32).astype(BF16), widen, preferred_element_type=F32)
        return jnp.sum(jnp.where(diagonal, wide, 0.0), axis=0, keepdims=True)

    for k in range(2):
        lanes[k:k + 1, :] = along(route_ref[k])
        place = place_ref[k] + 1
        lanes[2 + k:3 + k, :] = along(place & 255)
        lanes[4 + k:5 + k, :] = along(place >> 8)

    def freq_sq(rows):
        return jnp.where(rows < 128, rows, rows - 256).astype(F32)

    focus_row = info[0, 2:3, :]

    def weigh(c, carry):
        row = iota((128, HALF), 0)
        lane = iota((128, HALF), 1)
        row_f = freq_sq(tile * 16 + (row & 15))
        col_f = lane.astype(F32)
        radius = row_f * row_f + col_f * col_f
        focus = jnp.sum(jnp.where(lane == c * 8 + (row >> 4), focus_row, 0.0), axis=1, keepdims=True)
        contrast = -wave(focus * TURN * radius + PHASE)
        noise_here = jnp.concatenate([noise_ref[...]] * 8, axis=0)
        start = pl.multiple_of(c * 128, 128)
        pmo[pl.ds(start, 128), :] = (contrast * contrast * noise_here).astype(BF16)
        gain = contrast * noise_here
        rows = img_ref[pl.ds(start, 128), :].astype(F32)
        wi[pl.ds(start, 128), 0:HALF] = (gain * rows[:, :HALF]).astype(BF16)
        wi[pl.ds(start, 128), HALF:] = (gain * rows[:, HALF:]).astype(BF16)
        return carry

    lax.fori_loop(0, 8, weigh, 0)

    ia, ib = iota((256, 256), 0), iota((256, 256), 1)
    swap = jnp.where(((ia & 15) * 16 + (ia >> 4)) == ib, 1.0, 0.0).astype(BF16)
    for b in range(4):
        at = pl.multiple_of(core * PD + b * 16, 16)
        left = jnp.dot(swap, wi[b * 256:(b + 1) * 256, :], preferred_element_type=F32).astype(BF16)
        right = (-0.5 * jnp.dot(swap, pmo[b * 256:(b + 1) * 256, :], preferred_element_type=F32)).astype(BF16)
        for i in range(16):
            xw[pl.ds(at, 16), i * WIDE:i * WIDE + 256] = left[i * 16:(i + 1) * 16]
            xw[pl.ds(at, 16), i * WIDE + 256:(i + 1) * WIDE] = right[i * 16:(i + 1) * 16]

    pl.semaphore_wait(barrier, 22)
    lax.fori_loop(1, 8, vouch, 0)
    mate = jnp.bitwise_xor(dom, 1)
    mine = pl.ds(pl.multiple_of(core * PD, PD), PD)
    other = pl.ds(pl.multiple_of((1 - core) * PD, PD), PD)
    remote(xw.at[mine], xw.at[mine], pair(xw_sem), mate, tile).start()
    noise[0] = noise_ref[...]

    def small(u, carry):
        t = jnp.bitwise_xor(tile, u)
        remote(noise_ref, noise.at[u], pair(noise_sem), dom, t).start()
        return carry

    lax.fori_loop(1, 16, small, 0)

    def small_dom(e, carry):
        remote(info.at[0], info.at[e], pair(info_sem), jnp.bitwise_xor(dom, e), tile).start()
        return carry

    lax.fori_loop(1, 8, small_dom, 0)

    upper = jnp.where(ia < ib, 1.0, 0.0).astype(BF16)
    running = jnp.zeros((128, 1), F32)
    meta_low = jnp.zeros((128, 128), F32)
    meta_high = jnp.zeros((128, 128), F32)
    owner_id = iota((128, 256), 0)
    for k in range(2):
        for b in range(4):
            cols = slice(b * 256, (b + 1) * 256)
            owner = lanes[k:k + 1, cols].astype(I32)
            owner = ((owner & 15) << 3) | (owner >> 4)
            hit = jnp.where(owner_id == owner, 1.0, 0.0)
            hit16 = hit.astype(BF16)
            before = jnp.dot(hit16, upper, preferred_element_type=F32) + running
            rank = jnp.sum(hit * before, axis=0, keepdims=True)
            running = running + jnp.sum(hit, axis=1, keepdims=True)
            for t in range(16):
                ot[k, t, :, cols] = hit[t * 8:(t + 1) * 8]
            rank_ref[k:k + 1, cols] = rank
            number = iota((1, 256), 1) + b * 256
            group = owner_id >> 5
            same = (owner_id & 31).astype(F32) == rank
            low_value = jnp.where(group < 2, lanes[2 + k:3 + k, cols], (number & 255).astype(F32))
            high_value = jnp.where(group < 2, lanes[4 + k:5 + k, cols], ((number >> 8) + 4 * k).astype(F32))
            low16 = jnp.where(same, low_value, 0.0).astype(BF16)
            high16 = jnp.where(same, high_value, 0.0).astype(BF16)
            meta_low = meta_low + lax.dot_general(hit16, low16, NT, preferred_element_type=F32)
            meta_high = meta_high + lax.dot_general(hit16, high16, NT, preferred_element_type=F32)
    meta = meta_low + 256.0 * meta_high
    for t in range(16):
        for d in range(8):
            meta0[t, d] = meta[t * 8 + d:t * 8 + d + 1, :]
    slot_id = iota((32, MINE), 0).astype(F32)
    for k in range(2):
        mask_ref[k] = jnp.where(slot_id == rank_ref[k:k + 1, :], 1.0, 0.0).astype(BF16)

    meta1[0] = meta0[tile]

    def small_meta(u, carry):
        t = jnp.bitwise_xor(tile, u)
        remote(meta0.at[t], meta1.at[u], pair(m1_sem), dom, t).start()
        return carry

    lax.fori_loop(1, 16, small_meta, 0)

    def turn_of(i):
        return lax.rem(7 * (i + 1), 16)

    def pack(i, carry):
        blocks = []
        for e in range(8):
            t = jnp.bitwise_xor(tile, jnp.bitwise_xor(turn_of(i), SHIFT[e]))
            d = pl.ds(jnp.bitwise_xor(dom, e), 1)
            one = ot[0, t, d, :].astype(BF16)
            two = ot[1, t, d, :].astype(BF16)
            blocks.append(mask_ref[0] * one + mask_ref[1] * two)
        rows = jnp.dot(jnp.concatenate(blocks, axis=0), wi[...], preferred_element_type=F32).astype(BF16)
        for e in range(8):
            sb[i, e] = rows[e * 32:(e + 1) * 32]
        return carry

    pl.semaphore_wait(all_sem, 7)

    def ship(i, carry):
        for e in range(8):
            t = jnp.bitwise_xor(tile, jnp.bitwise_xor(turn_of(i), SHIFT[e]))
            d = jnp.bitwise_xor(dom, e)
            remote(sb.at[i, e], rb.at[i, e], (data_send, data_recv.at[i]), d, t).start()
        return carry

    def pack_ship(i, carry):
        pack(i, 0)
        return ship(i, 0)

    lax.fori_loop(0, FIRST, pack_ship, 0)

    wait_for(meta1.at[pl.ds(1, 15)], m1_sem.at[1])
    for u in range(16):
        meta2[0, u] = meta1[u, dom]

    def forward(e, carry):
        d = jnp.bitwise_xor(dom, e)
        remote(meta1.at[:, d], meta2.at[e], pair(m2_sem), d, tile).start()
        return carry

    lax.fori_loop(1, 8, forward, 0)

    wait_for(xw.at[other], xw_sem.at[1])
    row = tile // 4
    column = lax.rem(tile, 4)
    for c in range(REFS // CHUNK):
        loads(c).wait()

    def scored(i, carry):
        chunk = jnp.bitwise_xor(row, lax.rem(i + 1, 4))
        base = pl.multiple_of(chunk * CHUNK, CHUNK)

        def block(b, inner):
            refs = rv[pl.ds(base + b * 16, 16)].reshape(256, 256)
            turned = jnp.dot(swap, refs, preferred_element_type=F32)
            squares = (turned[:, :HALF] * turned[:, :HALF] + turned[:, HALF:] * turned[:, HALF:]).astype(BF16)
            turned = turned.astype(BF16)
            at = pl.multiple_of(b * 16, 16)
            for r in range(16):
                xc[pl.ds(at, 16), r * WIDE:r * WIDE + 256] = turned[r * 16:(r + 1) * 16]
                xc[pl.ds(at, 16), r * WIDE + 256:(r + 1) * WIDE] = squares[r * 16:(r + 1) * 16]
            return inner

        lax.fori_loop(0, CHUNK // 16, block, 0, unroll=8)
        score[pl.ds(base, CHUNK), :] = SCALE * lax.dot_general(xc[...], xw[...], NT, preferred_element_type=F32)

        def share(v, inner):
            t = chunk * 4 + jnp.bitwise_xor(column, v)
            u = jnp.bitwise_xor(t, tile)

            @pl.when(u != 0)
            def _():
                remote(score.at[pl.ds(pl.multiple_of(t * 64, 64), 64)], part.at[u], pair(part_sem), dom, t).start()

            return inner

        lax.fori_loop(0, 4, share, 0)
        return carry

    lax.fori_loop(0, 4, scored, 0)
    part[0] = score[pl.ds(pl.multiple_of(tile * 64, 64), 64), :]
    lax.fori_loop(FIRST, SECOND, pack_ship, 0)

    wait_for(info.at[pl.ds(1, 7)], info_sem.at[1])
    wait_for(noise.at[pl.ds(1, 15)], noise_sem.at[1])
    wait_for(meta2.at[pl.ds(1, 7)], m2_sem.at[1])
    lane1 = iota((1, HALF), 1)
    stack[...] = jnp.zeros_like(stack)
    for w in range(4):
        focus = jnp.where(lane1 < PD, info[2 * w, 2:3, :], info[2 * w + 1, 2:3, :])
        first = focus.astype(BF16).astype(F32)
        second = (focus - first).astype(BF16).astype(F32)
        stack[4 * w:4 * w + 1, :] = first
        stack[4 * w + 1:4 * w + 2, :] = second
        stack[4 * w + 2:4 * w + 3, :] = focus - first - second
    focus_rows = stack[...].astype(BF16)
    lane2 = iota((1, 256), 1)

    def prepare(i, carry):
        u = turn_of(i)
        quarter = lane1 >> 5
        strips, numbers = [], []
        for half in range(2):
            strip = jnp.zeros((1, HALF), F32)
            number = jnp.zeros((1, HALF), F32)
            for a in range(4):
                e = half * 4 + a
                got = meta2[e, jnp.bitwise_xor(u, SHIFT[e])]
                back = pltpu.roll(got, 64, 1)
                strip = jnp.where(quarter == a, got if a < 2 else back, strip)
                number = jnp.where(quarter == a, back if a < 2 else got, number)
            strips.append(strip)
            numbers.append(number)
        strip = jnp.concatenate(strips, axis=1).astype(I32) - 1
        number = jnp.concatenate(numbers, axis=1).astype(I32)
        low[i] = (strip & 255).astype(F32)
        high[i] = (strip >> 8).astype(F32)
        r = number & 15
        particle = ((number >> 4) & 63) + 64 * ((lane2 >> 5) & 1)
        code[i] = (particle + 128 * (number >> 10)).astype(F32)
        hot = jnp.where(iota((HALF, 256), 0) == particle, 1.0, 0.0).astype(BF16)
        found = jnp.dot(focus_rows, hot, preferred_element_type=F32)
        found = jnp.where((iota((16, 256), 0) >> 2) == (lane2 >> 6), found, 0.0)
        slope = jnp.sum(found, axis=0, keepdims=True) * TURN
        source = lane2 >> 5
        shift = ((source & 1) * 5) ^ (((source >> 1) & 1) * 10) ^ ((source >> 2) * 3)
        row_f = freq_sq((shift ^ jnp.bitwise_xor(tile, u)) * 16 + r)
        offset = slope * (row_f * row_f) + PHASE
        which = iota((8, 256), 0)
        rows = jnp.where(which == 0, slope, jnp.where(which == 1, offset, jnp.where(which == 2, (r + 16 * source).astype(F32), strip.astype(F32))))
        turned = jnp.transpose(rows)
        col_f = iota((256, HALF), 1).astype(F32)
        contrast = wave(turned[:, 0:1] * (col_f * col_f) + turned[:, 1:2])
        pick_row = jnp.where(iota((256, HALF), 1).astype(F32) == turned[:, 2:3], 1.0, 0.0).astype(BF16)
        pick_row = jnp.concatenate([pick_row] * 3, axis=1)
        full = jnp.concatenate([noise[jnp.bitwise_xor(u, SHIFT[e])] for e in range(8)], axis=0)
        first = full.astype(BF16)
        second = (full - first.astype(F32)).astype(BF16)
        third = (full - first.astype(F32) - second.astype(F32)).astype(BF16)
        gain = jnp.dot(pick_row, jnp.concatenate([first, second, third], axis=0), preferred_element_type=F32)
        power = contrast * contrast * gain
        upper_half = turned[:, 3:4] >= 1024.0
        pm[i, :, 0:HALF] = jnp.where(upper_half, 0.0, power).astype(BF16)
        pm[i, :, HALF:] = jnp.where(upper_half, power, 0.0).astype(BF16)
        return carry

    lax.fori_loop(0, 8, prepare, 0)

    wait_for(part.at[pl.ds(1, 15)], part_sem.at[1])
    total = part[0]
    for u in range(1, 16):
        total = total + part[u]
    same_core = jnp.where(core == 0, 0, 1)
    cand = []
    for k in range(2):
        zero = info[same_core, k:k + 1, :]
        one = info[1 - same_core, k:k + 1, :]
        cand.append(jnp.where(lane1 < PD, zero, one))
    ids = (iota((64, HALF), 0) + core * REFS + tile * 64).astype(F32)
    top = jnp.max(total, axis=0, keepdims=True)
    mass = jnp.sum(jnp.exp(total - top), axis=0, keepdims=True)
    got0 = jnp.sum(jnp.where(ids == cand[0], total, 0.0), axis=0, keepdims=True)
    got1 = jnp.sum(jnp.where(ids == cand[1], total, 0.0), axis=0, keepdims=True)
    which = iota((8, HALF), 0)
    stats[0] = jnp.where(which == 0, top, jnp.where(which == 1, mass, jnp.where(which == 2, got0, got1)))

    def tell(v, carry):
        d = jnp.bitwise_xor(dom, v // 16)
        t = jnp.bitwise_xor(tile, lax.rem(v, 16))
        remote(stats.at[0], stats.at[v], pair(stat_sem), d, t).start()
        return carry

    lax.fori_loop(1, 32, tell, 0)
    lax.fori_loop(SECOND, THIRD, pack_ship, 0)
    lax.fori_loop(8, 12, prepare, 0)
    wait_for(stats.at[pl.ds(1, 31)], stat_sem.at[1])
    every = stats[...]
    tops = every[:, 0, :]
    top = jnp.max(tops, axis=0, keepdims=True)
    mass = jnp.sum(every[:, 1, :] * jnp.exp(tops - top), axis=0, keepdims=True)
    got0 = jnp.sum(every[:, 2, :], axis=0, keepdims=True)
    got1 = jnp.sum(every[:, 3, :], axis=0, keepdims=True)
    spread = jnp.log(mass)
    best = jnp.maximum(got0, got1)
    raised0 = jnp.exp(got0 - best)
    raised1 = jnp.exp(got1 - best)
    chosen0 = raised0 / (raised0 + raised1)
    chosen1 = raised1 / (raised0 + raised1)
    rows = jnp.where(which == 0, chosen0, jnp.where(which == 1, chosen1, spread))
    rows = jnp.where(core == 0, rows, pltpu.roll(rows, 64, 1))
    picks[0] = rows
    spread_ref[...] = rows

    def pass_on(w, carry):
        remote(picks.at[0], picks.at[w], pair(pick_sem), jnp.bitwise_xor(dom, 2 * w), tile).start()
        return carry

    lax.fori_loop(1, 4, pass_on, 0)
    lax.fori_loop(THIRD, 15, pack_ship, 0)
    pack(15, 0)
    rb[15, 0] = sb[15, 0]

    for e in range(1, 8):
        t = jnp.bitwise_xor(tile, SHIFT[e])
        remote(sb.at[15, e], rb.at[15, e], (data_send, data_recv.at[15]), jnp.bitwise_xor(dom, e), t).start()
    lax.fori_loop(12, 16, prepare, 0)
    wait_for(picks.at[pl.ds(1, 3)], pick_sem.at[1])
    for w in range(4):
        table[2 * w:2 * w + 2, :] = picks[w, 0:2, :]
    chosen_rows = table[...].astype(BF16)

    def choose(u, carry):
        number = code[u].astype(I32)
        hot = jnp.where(iota((HALF, 256), 0) == (number & 127), 1.0, 0.0).astype(BF16)
        found = jnp.dot(chosen_rows, hot, preferred_element_type=F32)
        keep = iota((8, 256), 0) == ((lane2 >> 6) * 2 + (number >> 7))
        weight[u] = jnp.sum(jnp.where(keep, found, 0.0), axis=0, keepdims=True)
        return carry

    lax.fori_loop(0, 16, choose, 0)

    slab_row = iota((256, 4 * 256), 0).astype(F32).astype(BF16)
    for g in range(4):
        for i in range(4 * g, 4 * g + 4):
            if i == 15:
                wait_for(rb.at[15, pl.ds(1, 7)], data_recv.at[15])
            else:
                wait_for(rb.at[i], data_recv.at[i])
        low16 = jnp.concatenate([low[i] for i in range(4 * g, 4 * g + 4)], axis=1).astype(BF16)
        high_row = jnp.concatenate([high[i] for i in range(4 * g, 4 * g + 4)], axis=1)
        share_row = jnp.concatenate([weight[i] for i in range(4 * g, 4 * g + 4)], axis=1)

        def insert(b, carry):
            match = slab_row == low16
            rows = rb[4 * g:4 * g + 4].reshape(1024, 256)
            power = pm[4 * g:4 * g + 4].reshape(1024, 256)
            spots = []
            for h in range(2):
                value = jnp.where(high_row == (b + 4 * h).astype(F32), share_row, 0.0).astype(BF16)
                spots.append(jnp.where(match, value, jnp.zeros_like(value)))
            both = jnp.dot(spots[0] + spots[1], power, preferred_element_type=F32)
            for h in range(2):
                at = pl.ds(pl.multiple_of((b + 4 * h) * 256, 256), 256)
                data = jnp.dot(spots[h], rows, preferred_element_type=F32)
                more = both[:, h * HALF:(h + 1) * HALF]
                if g == 0:
                    vol_ref[at, 0:256] = data
                    vol_ref[at, 256:] = more
                else:
                    vol_ref[at, 0:256] += data
                    vol_ref[at, 256:] += more
            return carry

        lax.fori_loop(0, 4, insert, 0)

    wait_for(xw.at[mine], xw_sem.at[0])
    wait_for(meta1.at[pl.ds(1, 15)], m1_sem.at[0])
    wait_for(noise.at[pl.ds(1, 15)], noise_sem.at[0])
    wait_for(info.at[pl.ds(1, 7)], info_sem.at[0])
    wait_for(meta2.at[pl.ds(1, 7)], m2_sem.at[0])
    wait_for(part.at[pl.ds(1, 15)], part_sem.at[0])
    wait_for(stats.at[pl.ds(1, 31)], stat_sem.at[0])
    wait_for(picks.at[pl.ds(1, 3)], pick_sem.at[0])
    wait_for(sb.at[pl.ds(0, 15)], data_send)
    wait_for(sb.at[15, pl.ds(1, 7)], data_send)


def shards(images, defocus, noise_weight, references, candidates, route, strips):
    rows = images.reshape(MINE, 2 * HALF)
    focus = defocus[None]
    turned = [jnp.transpose(x[0, 0], (1, 2, 0)) for x in (route, strips)]
    vmem = pl.BlockSpec(memory_space=pltpu.VMEM)
    dma = pltpu.SemaphoreType.DMA
    volume, spread = pl.pallas_call(
        kernel,
        out_shape=(
            jax.ShapeDtypeStruct((STRIPS, WIDE), F32),
            jax.ShapeDtypeStruct((8, HALF), F32),
        ),
        in_specs=[vmem, vmem, vmem, vmem, pl.BlockSpec(memory_space=pl.ANY), vmem, vmem],
        out_specs=(vmem, vmem),
        scratch_shapes=[
            pltpu.VMEM((REFS, ROWS_DEV, 2 * HALF), BF16),
            pltpu.VMEM((CHUNK, DEPTH), BF16),
            pltpu.VMEM((2 * PD, DEPTH), BF16),
            pltpu.VMEM((MINE, 2 * HALF), BF16),
            pltpu.VMEM((MINE, HALF), BF16),
            pltpu.VMEM((2, 16, 8, MINE), F32),
            pltpu.VMEM((2, MINE), F32),
            pltpu.VMEM((2, 32, MINE), BF16),
            pltpu.VMEM((16, 8, 32, 256), BF16),
            pltpu.VMEM((16, 8, 32, 256), BF16),
            pltpu.VMEM((16, 8, 1, HALF), F32),
            pltpu.VMEM((16, 8, 1, HALF), F32),
            pltpu.VMEM((8, 16, 1, HALF), F32),
            pltpu.VMEM((8, MINE), F32),
            pltpu.VMEM((8, 8, HALF), F32),
            pltpu.VMEM((16, 16, HALF), F32),
            pltpu.VMEM((REFS, 2 * PD), F32),
            pltpu.VMEM((16, 64, 2 * PD), F32),
            pltpu.VMEM((32, 8, HALF), F32),
            pltpu.VMEM((4, 8, HALF), F32),
            pltpu.VMEM((16, HALF), F32),
            pltpu.VMEM((8, HALF), F32),
            pltpu.VMEM((16, 1, 256), F32),
            pltpu.VMEM((16, 1, 256), F32),
            pltpu.VMEM((16, 1, 256), F32),
            pltpu.VMEM((16, 1, 256), F32),
            pltpu.VMEM((16, 256, 256), BF16),
            dma((REFS // CHUNK,)),
            dma,
            dma((16,)),
            pltpu.SemaphoreType.REGULAR,
        ] + [dma((2,))] * 8,
        compiler_params=pltpu.CompilerParams(
            collective_id=0, has_side_effects=True, vmem_limit_bytes=56 << 20
        ),
    )(rows, focus, candidates.T, noise_weight, references, *turned)
    return volume, spread[2, :PD]


def solution(mesh):
    in_specs = (
        P("dom", "tile", None),
        P("dom"),
        P("tile", None),
        P(None, "tile", None),
        P("dom", None),
        P("dom", "tile", None, None, None),
        P("dom", "tile", None, None, None),
    )
    out_specs = (P(("dom", "tile"), None), P("dom"))
    return jax.shard_map(shards, mesh=mesh, in_specs=in_specs, out_specs=out_specs, check_vma=False)
```

```python
import math

import jax
import jax.numpy as jnp
from jax import lax
from jax.experimental import pallas as pl
from jax.experimental.pallas import tpu as pltpu
from jax.sharding import PartitionSpec as P

F32 = jnp.float32
BF16 = jnp.bfloat16
I32 = jnp.int32
MESH = pl.DeviceIdType.MESH
NT = (((1,), (1,)), ((), ()))

STRIPS = 2048
HALF = 128
ROWS_DEV = 16
PD = 64
MINE = PD * ROWS_DEV
NREF = 2048
REFS = NREF // 2
WIDE = 3 * HALF
DEPTH = ROWS_DEV * WIDE
CHUNK = 256
FIRST, SECOND, THIRD = 6, 8, 11
SHIFT = (0, 5, 10, 15, 3, 6, 9, 12)

TURN = 400.0 / 65536.0 / (2.0 * math.pi)
PHASE = 0.1 / (2.0 * math.pi)
SCALE = 1.0 / math.sqrt(32768.0)
SERIES = (
    6.283182793407029,
    -41.34141938561706,
    81.59613875538182,
    -76.5796878510169,
    41.20374363365668,
    -12.268859941003917,
)


def wave(turns):
    frac = turns - jnp.floor(turns + 0.5)
    sq = frac * frac
    total = jnp.full_like(sq, SERIES[-1])
    for coef in SERIES[-2::-1]:
        total = total * sq + coef
    return total * frac


def iota(shape, dim):
    return lax.broadcasted_iota(I32, shape, dim)


def kernel(
    img_ref, focus_ref, cand_ref, noise_ref, refs_ref, route_ref, place_ref,
    vol_ref, rows_ref, power_ref, label_ref, spread_ref,
    rv, xc, xw, wi, pmo, ot, rank_ref, mask_ref, sb, rb, meta0, meta1, meta2,
    lanes, info, noise, score, part, stats, picks, stack, table, low, high, code, weight, pm,
    ref_sem, data_send, data_recv, all_sem, xw_sem, info_sem, noise_sem, m1_sem, m2_sem, part_sem, stat_sem, pick_sem,
):
    dom = lax.axis_index("dom")
    tile = lax.axis_index("tile")
    core = lax.rem(dom, 2)
    barrier = pltpu.get_barrier_semaphore()

    def loads(c):
        return pltpu.make_async_copy(
            refs_ref.at[pl.ds(core * REFS + c * CHUNK, CHUNK)],
            rv.at[pl.ds(c * CHUNK, CHUNK)],
            ref_sem.at[c],
        )

    for c in range(REFS // CHUNK):
        loads(c).start()

    def greet_tile(u, carry):
        pl.semaphore_signal(barrier, inc=1, device_id=(dom, jnp.bitwise_xor(tile, u)), device_id_type=MESH)
        return carry

    def greet_dom(e, carry):
        pl.semaphore_signal(barrier, inc=1, device_id=(jnp.bitwise_xor(dom, e), tile), device_id_type=MESH)
        return carry

    def vouch(e, carry):
        pl.semaphore_signal(all_sem, inc=1, device_id=(jnp.bitwise_xor(dom, e), tile), device_id_type=MESH)
        return carry

    lax.fori_loop(1, 16, greet_tile, 0)
    lax.fori_loop(1, 8, greet_dom, 0)

    def remote(src, dst, sems, d, t):
        return pltpu.make_async_remote_copy(
            src_ref=src, dst_ref=dst, send_sem=sems[0], recv_sem=sems[1],
            device_id=(d, t), device_id_type=MESH,
        )

    def pair(sem):
        return sem.at[0], sem.at[1]

    def wait_for(ref, sem):
        pltpu.make_async_copy(ref, ref, sem).wait()

    info[0] = jnp.zeros((8, HALF), F32)
    for k in range(2):
        cand_row = cand_ref[k:k + 1, :].astype(F32)
        info[0, k:k + 1, :] = jnp.concatenate([cand_row, cand_row], axis=1)
    info[0, 2:3, :] = jnp.concatenate([focus_ref[...], focus_ref[...]], axis=1)
    widen = jnp.where((iota((PD, MINE), 1) >> 4) == iota((PD, MINE), 0), 1.0, 0.0).astype(BF16)
    diagonal = (iota((16, MINE), 1) & 15) == iota((16, MINE), 0)

    def along(block):
        wide = jnp.dot(block.astype(F32).astype(BF16), widen, preferred_element_type=F32)
        return jnp.sum(jnp.where(diagonal, wide, 0.0), axis=0, keepdims=True)

    for k in range(2):
        lanes[k:k + 1, :] = along(route_ref[k])
        place = place_ref[k] + 1
        lanes[2 + k:3 + k, :] = along(place & 255)
        lanes[4 + k:5 + k, :] = along(place >> 8)

    def freq_sq(rows):
        return jnp.where(rows < 128, rows, rows - 256).astype(F32)

    focus_row = info[0, 2:3, :]

    def weigh(c, carry):
        row = iota((128, HALF), 0)
        lane = iota((128, HALF), 1)
        row_f = freq_sq(tile * 16 + (row & 15))
        col_f = lane.astype(F32)
        radius = row_f * row_f + col_f * col_f
        focus = jnp.sum(jnp.where(lane == c * 8 + (row >> 4), focus_row, 0.0), axis=1, keepdims=True)
        contrast = -wave(focus * TURN * radius + PHASE)
        noise_here = jnp.concatenate([noise_ref[...]] * 8, axis=0)
        start = pl.multiple_of(c * 128, 128)
        pmo[pl.ds(start, 128), :] = (contrast * contrast * noise_here).astype(BF16)
        gain = contrast * noise_here
        rows = img_ref[pl.ds(start, 128), :].astype(F32)
        wi[pl.ds(start, 128), 0:HALF] = (gain * rows[:, :HALF]).astype(BF16)
        wi[pl.ds(start, 128), HALF:] = (gain * rows[:, HALF:]).astype(BF16)
        return carry

    lax.fori_loop(0, 8, weigh, 0)

    ia, ib = iota((256, 256), 0), iota((256, 256), 1)
    swap = jnp.where(((ia & 15) * 16 + (ia >> 4)) == ib, 1.0, 0.0).astype(BF16)
    for b in range(4):
        at = pl.multiple_of(core * PD + b * 16, 16)
        left = jnp.dot(swap, wi[b * 256:(b + 1) * 256, :], preferred_element_type=F32).astype(BF16)
        right = (-0.5 * jnp.dot(swap, pmo[b * 256:(b + 1) * 256, :], preferred_element_type=F32)).astype(BF16)
        for i in range(16):
            xw[pl.ds(at, 16), i * WIDE:i * WIDE + 256] = left[i * 16:(i + 1) * 16]
            xw[pl.ds(at, 16), i * WIDE + 256:(i + 1) * WIDE] = right[i * 16:(i + 1) * 16]

    pl.semaphore_wait(barrier, 22)
    lax.fori_loop(1, 8, vouch, 0)
    mate = jnp.bitwise_xor(dom, 1)
    mine = pl.ds(pl.multiple_of(core * PD, PD), PD)
    other = pl.ds(pl.multiple_of((1 - core) * PD, PD), PD)
    remote(xw.at[mine], xw.at[mine], pair(xw_sem), mate, tile).start()
    noise[0] = noise_ref[...]

    def small(u, carry):
        t = jnp.bitwise_xor(tile, u)
        remote(noise_ref, noise.at[u], pair(noise_sem), dom, t).start()
        return carry

    lax.fori_loop(1, 16, small, 0)

    def small_dom(e, carry):
        remote(info.at[0], info.at[e], pair(info_sem), jnp.bitwise_xor(dom, e), tile).start()
        return carry

    lax.fori_loop(1, 8, small_dom, 0)

    upper = jnp.where(ia < ib, 1.0, 0.0).astype(BF16)
    running = jnp.zeros((128, 1), F32)
    meta_low = jnp.zeros((128, 128), F32)
    meta_high = jnp.zeros((128, 128), F32)
    owner_id = iota((128, 256), 0)
    for k in range(2):
        for b in range(4):
            cols = slice(b * 256, (b + 1) * 256)
            owner = lanes[k:k + 1, cols].astype(I32)
            owner = ((owner & 15) << 3) | (owner >> 4)
            hit = jnp.where(owner_id == owner, 1.0, 0.0)
            hit16 = hit.astype(BF16)
            before = jnp.dot(hit16, upper, preferred_element_type=F32) + running
            rank = jnp.sum(hit * before, axis=0, keepdims=True)
            running = running + jnp.sum(hit, axis=1, keepdims=True)
            for t in range(16):
                ot[k, t, :, cols] = hit[t * 8:(t + 1) * 8]
            rank_ref[k:k + 1, cols] = rank
            number = iota((1, 256), 1) + b * 256
            group = owner_id >> 5
            same = (owner_id & 31).astype(F32) == rank
            low_value = jnp.where(group < 2, lanes[2 + k:3 + k, cols], (number & 255).astype(F32))
            high_value = jnp.where(group < 2, lanes[4 + k:5 + k, cols], ((number >> 8) + 4 * k).astype(F32))
            low16 = jnp.where(same, low_value, 0.0).astype(BF16)
            high16 = jnp.where(same, high_value, 0.0).astype(BF16)
            meta_low = meta_low + lax.dot_general(hit16, low16, NT, preferred_element_type=F32)
            meta_high = meta_high + lax.dot_general(hit16, high16, NT, preferred_element_type=F32)
    meta = meta_low + 256.0 * meta_high
    for t in range(16):
        for d in range(8):
            meta0[t, d] = meta[t * 8 + d:t * 8 + d + 1, :]
    slot_id = iota((32, MINE), 0).astype(F32)
    for k in range(2):
        mask_ref[k] = jnp.where(slot_id == rank_ref[k:k + 1, :], 1.0, 0.0).astype(BF16)

    meta1[0] = meta0[tile]

    def small_meta(u, carry):
        t = jnp.bitwise_xor(tile, u)
        remote(meta0.at[t], meta1.at[u], pair(m1_sem), dom, t).start()
        return carry

    lax.fori_loop(1, 16, small_meta, 0)

    def turn_of(i):
        return lax.rem(7 * (i + 1), 16)

    def pack(i, carry):
        blocks = []
        for e in range(8):
            t = jnp.bitwise_xor(tile, jnp.bitwise_xor(turn_of(i), SHIFT[e]))
            d = pl.ds(jnp.bitwise_xor(dom, e), 1)
            one = ot[0, t, d, :].astype(BF16)
            two = ot[1, t, d, :].astype(BF16)
            blocks.append(mask_ref[0] * one + mask_ref[1] * two)
        rows = jnp.dot(jnp.concatenate(blocks, axis=0), wi[...], preferred_element_type=F32).astype(BF16)
        for e in range(8):
            sb[i, e] = rows[e * 32:(e + 1) * 32]
        return carry

    pl.semaphore_wait(all_sem, 7)

    def ship(i, carry):
        for e in range(8):
            t = jnp.bitwise_xor(tile, jnp.bitwise_xor(turn_of(i), SHIFT[e]))
            d = jnp.bitwise_xor(dom, e)
            remote(sb.at[i, e], rb.at[i, e], (data_send, data_recv.at[i]), d, t).start()
        return carry

    def pack_ship(i, carry):
        pack(i, 0)
        return ship(i, 0)

    lax.fori_loop(0, FIRST, pack_ship, 0)

    wait_for(meta1.at[pl.ds(1, 15)], m1_sem.at[1])
    for u in range(16):
        meta2[0, u] = meta1[u, dom]

    def forward(e, carry):
        d = jnp.bitwise_xor(dom, e)
        remote(meta1.at[:, d], meta2.at[e], pair(m2_sem), d, tile).start()
        return carry

    lax.fori_loop(1, 8, forward, 0)

    wait_for(xw.at[other], xw_sem.at[1])
    row = tile // 4
    column = lax.rem(tile, 4)
    for c in range(REFS // CHUNK):
        loads(c).wait()

    def scored(i, carry):
        chunk = jnp.bitwise_xor(row, lax.rem(i + 1, 4))
        base = pl.multiple_of(chunk * CHUNK, CHUNK)

        def block(b, inner):
            refs = rv[pl.ds(base + b * 16, 16)].reshape(256, 256)
            turned = jnp.dot(swap, refs, preferred_element_type=F32)
            squares = (turned[:, :HALF] * turned[:, :HALF] + turned[:, HALF:] * turned[:, HALF:]).astype(BF16)
            turned = turned.astype(BF16)
            at = pl.multiple_of(b * 16, 16)
            for r in range(16):
                xc[pl.ds(at, 16), r * WIDE:r * WIDE + 256] = turned[r * 16:(r + 1) * 16]
                xc[pl.ds(at, 16), r * WIDE + 256:(r + 1) * WIDE] = squares[r * 16:(r + 1) * 16]
            return inner

        lax.fori_loop(0, CHUNK // 16, block, 0, unroll=8)
        score[pl.ds(base, CHUNK), :] = SCALE * lax.dot_general(xc[...], xw[...], NT, preferred_element_type=F32)

        def share(v, inner):
            t = chunk * 4 + jnp.bitwise_xor(column, v)
            u = jnp.bitwise_xor(t, tile)

            @pl.when(u != 0)
            def _():
                remote(score.at[pl.ds(pl.multiple_of(t * 64, 64), 64)], part.at[u], pair(part_sem), dom, t).start()

            return inner

        lax.fori_loop(0, 4, share, 0)
        return carry

    lax.fori_loop(0, 4, scored, 0)
    part[0] = score[pl.ds(pl.multiple_of(tile * 64, 64), 64), :]
    lax.fori_loop(FIRST, SECOND, pack_ship, 0)

    wait_for(info.at[pl.ds(1, 7)], info_sem.at[1])
    wait_for(noise.at[pl.ds(1, 15)], noise_sem.at[1])
    wait_for(meta2.at[pl.ds(1, 7)], m2_sem.at[1])
    lane1 = iota((1, HALF), 1)
    stack[...] = jnp.zeros_like(stack)
    for w in range(4):
        focus = jnp.where(lane1 < PD, info[2 * w, 2:3, :], info[2 * w + 1, 2:3, :])
        first = focus.astype(BF16).astype(F32)
        second = (focus - first).astype(BF16).astype(F32)
        stack[4 * w:4 * w + 1, :] = first
        stack[4 * w + 1:4 * w + 2, :] = second
        stack[4 * w + 2:4 * w + 3, :] = focus - first - second
    focus_rows = stack[...].astype(BF16)
    lane2 = iota((1, 256), 1)

    def prepare(i, carry):
        u = turn_of(i)
        quarter = lane1 >> 5
        strips, numbers = [], []
        for half in range(2):
            strip = jnp.zeros((1, HALF), F32)
            number = jnp.zeros((1, HALF), F32)
            for a in range(4):
                e = half * 4 + a
                got = meta2[e, jnp.bitwise_xor(u, SHIFT[e])]
                back = pltpu.roll(got, 64, 1)
                strip = jnp.where(quarter == a, got if a < 2 else back, strip)
                number = jnp.where(quarter == a, back if a < 2 else got, number)
            strips.append(strip)
            numbers.append(number)
        strip = jnp.concatenate(strips, axis=1).astype(I32) - 1
        number = jnp.concatenate(numbers, axis=1).astype(I32)
        low[i] = (strip & 255).astype(F32)
        high[i] = (strip >> 8).astype(F32)
        r = number & 15
        particle = ((number >> 4) & 63) + 64 * ((lane2 >> 5) & 1)
        code[i] = (particle + 128 * (number >> 10)).astype(F32)
        hot = jnp.where(iota((HALF, 256), 0) == particle, 1.0, 0.0).astype(BF16)
        found = jnp.dot(focus_rows, hot, preferred_element_type=F32)
        found = jnp.where((iota((16, 256), 0) >> 2) == (lane2 >> 6), found, 0.0)
        slope = jnp.sum(found, axis=0, keepdims=True) * TURN
        source = lane2 >> 5
        shift = ((source & 1) * 5) ^ (((source >> 1) & 1) * 10) ^ ((source >> 2) * 3)
        row_f = freq_sq((shift ^ jnp.bitwise_xor(tile, u)) * 16 + r)
        offset = slope * (row_f * row_f) + PHASE
        which = iota((8, 256), 0)
        rows = jnp.where(which == 0, slope, jnp.where(which == 1, offset, jnp.where(which == 2, (r + 16 * source).astype(F32), strip.astype(F32))))
        turned = jnp.transpose(rows)
        col_f = iota((256, HALF), 1).astype(F32)
        contrast = wave(turned[:, 0:1] * (col_f * col_f) + turned[:, 1:2])
        pick_row = jnp.where(iota((256, HALF), 1).astype(F32) == turned[:, 2:3], 1.0, 0.0).astype(BF16)
        pick_row = jnp.concatenate([pick_row] * 3, axis=1)
        full = jnp.concatenate([noise[jnp.bitwise_xor(u, SHIFT[e])] for e in range(8)], axis=0)
        first = full.astype(BF16)
        second = (full - first.astype(F32)).astype(BF16)
        third = (full - first.astype(F32) - second.astype(F32)).astype(BF16)
        gain = jnp.dot(pick_row, jnp.concatenate([first, second, third], axis=0), preferred_element_type=F32)
        power = contrast * contrast * gain
        upper_half = turned[:, 3:4] >= 1024.0
        pm[i, :, 0:HALF] = jnp.where(upper_half, 0.0, power).astype(BF16)
        pm[i, :, HALF:] = jnp.where(upper_half, power, 0.0).astype(BF16)
        return carry

    lax.fori_loop(0, 8, prepare, 0)

    wait_for(part.at[pl.ds(1, 15)], part_sem.at[1])
    total = part[0]
    for u in range(1, 16):
        total = total + part[u]
    same_core = jnp.where(core == 0, 0, 1)
    cand = []
    for k in range(2):
        zero = info[same_core, k:k + 1, :]
        one = info[1 - same_core, k:k + 1, :]
        cand.append(jnp.where(lane1 < PD, zero, one))
    ids = (iota((64, HALF), 0) + core * REFS + tile * 64).astype(F32)
    top = jnp.max(total, axis=0, keepdims=True)
    mass = jnp.sum(jnp.exp(total - top), axis=0, keepdims=True)
    got0 = jnp.sum(jnp.where(ids == cand[0], total, 0.0), axis=0, keepdims=True)
    got1 = jnp.sum(jnp.where(ids == cand[1], total, 0.0), axis=0, keepdims=True)
    which = iota((8, HALF), 0)
    stats[0] = jnp.where(which == 0, top, jnp.where(which == 1, mass, jnp.where(which == 2, got0, got1)))

    def tell(v, carry):
        d = jnp.bitwise_xor(dom, v // 16)
        t = jnp.bitwise_xor(tile, lax.rem(v, 16))
        remote(stats.at[0], stats.at[v], pair(stat_sem), d, t).start()
        return carry

    lax.fori_loop(1, 32, tell, 0)
    lax.fori_loop(SECOND, THIRD, pack_ship, 0)
    lax.fori_loop(8, 12, prepare, 0)
    wait_for(stats.at[pl.ds(1, 31)], stat_sem.at[1])
    every = stats[...]
    tops = every[:, 0, :]
    top = jnp.max(tops, axis=0, keepdims=True)
    mass = jnp.sum(every[:, 1, :] * jnp.exp(tops - top), axis=0, keepdims=True)
    got0 = jnp.sum(every[:, 2, :], axis=0, keepdims=True)
    got1 = jnp.sum(every[:, 3, :], axis=0, keepdims=True)
    spread = jnp.log(mass)
    best = jnp.maximum(got0, got1)
    raised0 = jnp.exp(got0 - best)
    raised1 = jnp.exp(got1 - best)
    chosen0 = raised0 / (raised0 + raised1)
    chosen1 = raised1 / (raised0 + raised1)
    rows = jnp.where(which == 0, chosen0, jnp.where(which == 1, chosen1, spread))
    rows = jnp.where(core == 0, rows, pltpu.roll(rows, 64, 1))
    picks[0] = rows
    spread_ref[...] = rows

    def pass_on(w, carry):
        remote(picks.at[0], picks.at[w], pair(pick_sem), jnp.bitwise_xor(dom, 2 * w), tile).start()
        return carry

    lax.fori_loop(1, 4, pass_on, 0)
    lax.fori_loop(THIRD, 15, pack_ship, 0)
    pack(15, 0)
    rb[15, 0] = sb[15, 0]

    for e in range(1, 8):
        t = jnp.bitwise_xor(tile, SHIFT[e])
        remote(sb.at[15, e], rb.at[15, e], (data_send, data_recv.at[15]), jnp.bitwise_xor(dom, e), t).start()
    lax.fori_loop(12, 16, prepare, 0)
    wait_for(picks.at[pl.ds(1, 3)], pick_sem.at[1])
    for w in range(4):
        table[2 * w:2 * w + 2, :] = picks[w, 0:2, :]
    chosen_rows = table[...].astype(BF16)

    def choose(u, carry):
        number = code[u].astype(I32)
        hot = jnp.where(iota((HALF, 256), 0) == (number & 127), 1.0, 0.0).astype(BF16)
        found = jnp.dot(chosen_rows, hot, preferred_element_type=F32)
        keep = iota((8, 256), 0) == ((lane2 >> 6) * 2 + (number >> 7))
        weight[u] = jnp.sum(jnp.where(keep, found, 0.0), axis=0, keepdims=True)
        return carry

    lax.fori_loop(0, 16, choose, 0)

    slab_row = iota((256, 4 * 256), 0).astype(F32).astype(BF16)
    for g in range(4):
        for i in range(4 * g, 4 * g + 4):
            if i == 15:
                wait_for(rb.at[15, pl.ds(1, 7)], data_recv.at[15])
            else:
                wait_for(rb.at[i], data_recv.at[i])
        low_row = jnp.concatenate([low[i] for i in range(4 * g, 4 * g + 4)], axis=1)
        high_row = jnp.concatenate([high[i] for i in range(4 * g, 4 * g + 4)], axis=1)
        share_row = jnp.concatenate([weight[i] for i in range(4 * g, 4 * g + 4)], axis=1)
        if g == 3:
            rows_ref[...] = rb[12:16].reshape(1024, 256)
            power_ref[...] = pm[12:16].reshape(1024, 256)
            label_ref[0:1, :] = low_row
            label_ref[1:2, :] = high_row
            label_ref[2:3, :] = share_row
            break
        low16 = low_row.astype(BF16)

        def insert(b, carry):
            match = slab_row == low16
            rows = rb[4 * g:4 * g + 4].reshape(1024, 256)
            power = pm[4 * g:4 * g + 4].reshape(1024, 256)
            spots = []
            for h in range(2):
                value = jnp.where(high_row == (b + 4 * h).astype(F32), share_row, 0.0).astype(BF16)
                spots.append(jnp.where(match, value, jnp.zeros_like(value)))
            both = jnp.dot(spots[0] + spots[1], power, preferred_element_type=F32)
            for h in range(2):
                at = pl.ds(pl.multiple_of((b + 4 * h) * 256, 256), 256)
                data = jnp.dot(spots[h], rows, preferred_element_type=F32)
                more = both[:, h * HALF:(h + 1) * HALF]
                if g == 0:
                    vol_ref[at, 0:256] = data
                    vol_ref[at, 256:] = more
                else:
                    vol_ref[at, 0:256] += data
                    vol_ref[at, 256:] += more
            return carry

        lax.fori_loop(0, 4, insert, 0)

    wait_for(xw.at[mine], xw_sem.at[0])
    wait_for(meta1.at[pl.ds(1, 15)], m1_sem.at[0])
    wait_for(noise.at[pl.ds(1, 15)], noise_sem.at[0])
    wait_for(info.at[pl.ds(1, 7)], info_sem.at[0])
    wait_for(meta2.at[pl.ds(1, 7)], m2_sem.at[0])
    wait_for(part.at[pl.ds(1, 15)], part_sem.at[0])
    wait_for(stats.at[pl.ds(1, 31)], stat_sem.at[0])
    wait_for(picks.at[pl.ds(1, 3)], pick_sem.at[0])
    wait_for(sb.at[pl.ds(0, 15)], data_send)
    wait_for(sb.at[15, pl.ds(1, 7)], data_send)


def finish(part_ref, rows_ref, power_ref, label_ref, stat_ref, vol_ref, spread_ref):
    b = pl.program_id(0)
    match = iota((256, 1024), 0).astype(F32).astype(BF16) == label_ref[0:1, :].astype(BF16)
    spots = []
    for h in range(2):
        value = jnp.where(label_ref[1:2, :] == (b + 4 * h).astype(F32), label_ref[2:3, :], 0.0).astype(BF16)
        spots.append(jnp.where(match, value, jnp.zeros_like(value)))
    both = jnp.dot(spots[0] + spots[1], power_ref[...], preferred_element_type=F32)
    for h in range(2):
        data = jnp.dot(spots[h], rows_ref[...], preferred_element_type=F32)
        vol_ref[h, :, 0:256] = part_ref[h, :, 0:256] + data
        vol_ref[h, :, 256:] = part_ref[h, :, 256:] + both[:, h * HALF:(h + 1) * HALF]
    spread_ref[...] = stat_ref[2:3, 0:PD]


def shards(images, defocus, noise_weight, references, candidates, route, strips):
    rows = images.reshape(MINE, 2 * HALF)
    focus = defocus[None]
    turned = [jnp.transpose(x[0, 0], (1, 2, 0)) for x in (route, strips)]
    vmem = pl.BlockSpec(memory_space=pltpu.VMEM)
    dma = pltpu.SemaphoreType.DMA
    partial, last_rows, last_power, labels, stat = pl.pallas_call(
        kernel,
        out_shape=(
            jax.ShapeDtypeStruct((STRIPS, WIDE), F32),
            jax.ShapeDtypeStruct((1024, 256), BF16),
            jax.ShapeDtypeStruct((1024, 256), BF16),
            jax.ShapeDtypeStruct((8, 1024), F32),
            jax.ShapeDtypeStruct((8, HALF), F32),
        ),
        in_specs=[vmem, vmem, vmem, vmem, pl.BlockSpec(memory_space=pl.ANY), vmem, vmem],
        out_specs=(vmem,) * 5,
        scratch_shapes=[
            pltpu.VMEM((REFS, ROWS_DEV, 2 * HALF), BF16),
            pltpu.VMEM((CHUNK, DEPTH), BF16),
            pltpu.VMEM((2 * PD, DEPTH), BF16),
            pltpu.VMEM((MINE, 2 * HALF), BF16),
            pltpu.VMEM((MINE, HALF), BF16),
            pltpu.VMEM((2, 16, 8, MINE), F32),
            pltpu.VMEM((2, MINE), F32),
            pltpu.VMEM((2, 32, MINE), BF16),
            pltpu.VMEM((16, 8, 32, 256), BF16),
            pltpu.VMEM((16, 8, 32, 256), BF16),
            pltpu.VMEM((16, 8, 1, HALF), F32),
            pltpu.VMEM((16, 8, 1, HALF), F32),
            pltpu.VMEM((8, 16, 1, HALF), F32),
            pltpu.VMEM((8, MINE), F32),
            pltpu.VMEM((8, 8, HALF), F32),
            pltpu.VMEM((16, 16, HALF), F32),
            pltpu.VMEM((REFS, 2 * PD), F32),
            pltpu.VMEM((16, 64, 2 * PD), F32),
            pltpu.VMEM((32, 8, HALF), F32),
            pltpu.VMEM((4, 8, HALF), F32),
            pltpu.VMEM((16, HALF), F32),
            pltpu.VMEM((8, HALF), F32),
            pltpu.VMEM((16, 1, 256), F32),
            pltpu.VMEM((16, 1, 256), F32),
            pltpu.VMEM((16, 1, 256), F32),
            pltpu.VMEM((16, 1, 256), F32),
            pltpu.VMEM((16, 256, 256), BF16),
            dma((REFS // CHUNK,)),
            dma,
            dma((16,)),
            pltpu.SemaphoreType.REGULAR,
        ] + [dma((2,))] * 8,
        compiler_params=pltpu.CompilerParams(
            collective_id=0, has_side_effects=True, vmem_limit_bytes=56 << 20
        ),
    )(rows, focus, candidates.T, noise_weight, references, *turned)
    half = pl.BlockSpec((2, 256, WIDE), lambda b: (0, b, 0))

    def whole(shape):
        return pl.BlockSpec(shape, lambda b: (0, 0))

    volume, spread = pl.pallas_call(
        finish,
        grid=(4,),
        out_shape=(
            jax.ShapeDtypeStruct((2, STRIPS // 2, WIDE), F32),
            jax.ShapeDtypeStruct((1, PD), F32),
        ),
        in_specs=[half, whole((1024, 256)), whole((1024, 256)), whole((8, 1024)), whole((8, HALF))],
        out_specs=(half, whole((1, PD))),
        compiler_params=pltpu.CompilerParams(vmem_limit_bytes=62 << 20),
    )(partial.reshape(2, STRIPS // 2, WIDE), last_rows, last_power, labels, stat)
    return volume.reshape(STRIPS, WIDE), spread[0]


def solution(mesh):
    in_specs = (
        P("dom", "tile", None),
        P("dom"),
        P("tile", None),
        P(None, "tile", None),
        P("dom", None),
        P("dom", "tile", None, None, None),
        P("dom", "tile", None, None, None),
    )
    out_specs = (P(("dom", "tile"), None), P("dom"))
    return jax.shard_map(shards, mesh=mesh, in_specs=in_specs, out_specs=out_specs, check_vma=False)
```

```python
import math

import jax
import jax.numpy as jnp
from jax import lax
from jax.experimental import pallas as pl
from jax.experimental.pallas import tpu as pltpu
from jax.sharding import PartitionSpec as P

F32 = jnp.float32
BF16 = jnp.bfloat16
I32 = jnp.int32
MESH = pl.DeviceIdType.MESH
NT = (((1,), (1,)), ((), ()))

STRIPS = 2048
HALF = 128
ROWS_DEV = 16
PD = 64
MINE = PD * ROWS_DEV
NREF = 2048
REFS = NREF // 2
WIDE = 3 * HALF
DEPTH = ROWS_DEV * WIDE
CHUNK = 256
FIRST, SECOND, THIRD = 6, 8, 11
SHIFT = (0, 5, 10, 15, 3, 6, 9, 12)

TURN = 400.0 / 65536.0 / (2.0 * math.pi)
PHASE = 0.1 / (2.0 * math.pi)
SCALE = 1.0 / math.sqrt(32768.0)
SERIES = (
    6.283182793407029,
    -41.34141938561706,
    81.59613875538182,
    -76.5796878510169,
    41.20374363365668,
    -12.268859941003917,
)


def wave(turns):
    frac = turns - jnp.floor(turns + 0.5)
    sq = frac * frac
    total = jnp.full_like(sq, SERIES[-1])
    for coef in SERIES[-2::-1]:
        total = total * sq + coef
    return total * frac


def iota(shape, dim):
    return lax.broadcasted_iota(I32, shape, dim)


def kernel(
    img_ref, focus_ref, cand_ref, noise_ref, refs_ref, route_ref, place_ref,
    vol_ref, rows_ref, power_ref, label_ref, spread_ref,
    rv, xc, xw, wi, pmo, ot, rank_ref, mask_ref, sb, rb, meta0, meta1, meta2,
    lanes, info, noise, score, part, stats, picks, stack, table, low, high, code, weight, pm,
    ref_sem, data_send, data_recv, all_sem, xw_sem, info_sem, noise_sem, m1_sem, m2_sem, part_sem, stat_sem, pick_sem,
):
    dom = lax.axis_index("dom")
    tile = lax.axis_index("tile")
    core = lax.rem(dom, 2)
    barrier = pltpu.get_barrier_semaphore()

    def loads(c):
        return pltpu.make_async_copy(
            refs_ref.at[pl.ds(core * REFS + c * CHUNK, CHUNK)],
            rv.at[pl.ds(c * CHUNK, CHUNK)],
            ref_sem.at[c],
        )

    for c in range(REFS // CHUNK):
        loads(c).start()

    def greet_tile(u, carry):
        pl.semaphore_signal(barrier, inc=1, device_id=(dom, jnp.bitwise_xor(tile, u)), device_id_type=MESH)
        return carry

    def greet_dom(e, carry):
        pl.semaphore_signal(barrier, inc=1, device_id=(jnp.bitwise_xor(dom, e), tile), device_id_type=MESH)
        return carry

    def vouch(e, carry):
        pl.semaphore_signal(all_sem, inc=1, device_id=(jnp.bitwise_xor(dom, e), tile), device_id_type=MESH)
        return carry

    lax.fori_loop(1, 16, greet_tile, 0)
    lax.fori_loop(1, 8, greet_dom, 0)

    def remote(src, dst, sems, d, t):
        return pltpu.make_async_remote_copy(
            src_ref=src, dst_ref=dst, send_sem=sems[0], recv_sem=sems[1],
            device_id=(d, t), device_id_type=MESH,
        )

    def pair(sem):
        return sem.at[0], sem.at[1]

    def wait_for(ref, sem):
        pltpu.make_async_copy(ref, ref, sem).wait()

    info[0] = jnp.zeros((8, HALF), F32)
    for k in range(2):
        cand_row = cand_ref[k:k + 1, :].astype(F32)
        info[0, k:k + 1, :] = jnp.concatenate([cand_row, cand_row], axis=1)
    info[0, 2:3, :] = jnp.concatenate([focus_ref[...], focus_ref[...]], axis=1)
    widen = jnp.where((iota((PD, MINE), 1) >> 4) == iota((PD, MINE), 0), 1.0, 0.0).astype(BF16)
    diagonal = (iota((16, MINE), 1) & 15) == iota((16, MINE), 0)

    def along(block):
        wide = jnp.dot(block.astype(F32).astype(BF16), widen, preferred_element_type=F32)
        return jnp.sum(jnp.where(diagonal, wide, 0.0), axis=0, keepdims=True)

    for k in range(2):
        lanes[k:k + 1, :] = along(route_ref[k])
        place = place_ref[k] + 1
        lanes[2 + k:3 + k, :] = along(place & 255)
        lanes[4 + k:5 + k, :] = along(place >> 8)

    def freq_sq(rows):
        return jnp.where(rows < 128, rows, rows - 256).astype(F32)

    focus_row = info[0, 2:3, :]

    def weigh(c, carry):
        row = iota((128, HALF), 0)
        lane = iota((128, HALF), 1)
        row_f = freq_sq(tile * 16 + (row & 15))
        col_f = lane.astype(F32)
        radius = row_f * row_f + col_f * col_f
        focus = jnp.sum(jnp.where(lane == c * 8 + (row >> 4), focus_row, 0.0), axis=1, keepdims=True)
        contrast = -wave(focus * TURN * radius + PHASE)
        noise_here = jnp.concatenate([noise_ref[...]] * 8, axis=0)
        start = pl.multiple_of(c * 128, 128)
        pmo[pl.ds(start, 128), :] = (contrast * contrast * noise_here).astype(BF16)
        gain = contrast * noise_here
        rows = img_ref[pl.ds(start, 128), :].astype(F32)
        wi[pl.ds(start, 128), 0:HALF] = (gain * rows[:, :HALF]).astype(BF16)
        wi[pl.ds(start, 128), HALF:] = (gain * rows[:, HALF:]).astype(BF16)
        return carry

    lax.fori_loop(0, 8, weigh, 0)

    ia, ib = iota((256, 256), 0), iota((256, 256), 1)
    swap = jnp.where(((ia & 15) * 16 + (ia >> 4)) == ib, 1.0, 0.0).astype(BF16)
    for b in range(4):
        at = pl.multiple_of(core * PD + b * 16, 16)
        left = jnp.dot(swap, wi[b * 256:(b + 1) * 256, :], preferred_element_type=F32).astype(BF16)
        right = (-0.5 * jnp.dot(swap, pmo[b * 256:(b + 1) * 256, :], preferred_element_type=F32)).astype(BF16)
        for i in range(16):
            xw[pl.ds(at, 16), i * WIDE:i * WIDE + 256] = left[i * 16:(i + 1) * 16]
            xw[pl.ds(at, 16), i * WIDE + 256:(i + 1) * WIDE] = right[i * 16:(i + 1) * 16]

    pl.semaphore_wait(barrier, 22)
    lax.fori_loop(1, 8, vouch, 0)
    mate = jnp.bitwise_xor(dom, 1)
    mine = pl.ds(pl.multiple_of(core * PD, PD), PD)
    other = pl.ds(pl.multiple_of((1 - core) * PD, PD), PD)
    remote(xw.at[mine], xw.at[mine], pair(xw_sem), mate, tile).start()
    noise[0] = noise_ref[...]

    def small(u, carry):
        t = jnp.bitwise_xor(tile, u)
        remote(noise_ref, noise.at[u], pair(noise_sem), dom, t).start()
        return carry

    lax.fori_loop(1, 16, small, 0)

    def small_dom(e, carry):
        remote(info.at[0], info.at[e], pair(info_sem), jnp.bitwise_xor(dom, e), tile).start()
        return carry

    lax.fori_loop(1, 8, small_dom, 0)

    upper = jnp.where(ia < ib, 1.0, 0.0).astype(BF16)
    running = jnp.zeros((128, 1), F32)
    meta_low = jnp.zeros((128, 128), F32)
    meta_high = jnp.zeros((128, 128), F32)
    owner_id = iota((128, 256), 0)
    for k in range(2):
        for b in range(4):
            cols = slice(b * 256, (b + 1) * 256)
            owner = lanes[k:k + 1, cols].astype(I32)
            owner = ((owner & 15) << 3) | (owner >> 4)
            hit = jnp.where(owner_id == owner, 1.0, 0.0)
            hit16 = hit.astype(BF16)
            before = jnp.dot(hit16, upper, preferred_element_type=F32) + running
            rank = jnp.sum(hit * before, axis=0, keepdims=True)
            running = running + jnp.sum(hit, axis=1, keepdims=True)
            for t in range(16):
                ot[k, t, :, cols] = hit[t * 8:(t + 1) * 8]
            rank_ref[k:k + 1, cols] = rank
            number = iota((1, 256), 1) + b * 256
            group = owner_id >> 5
            same = (owner_id & 31).astype(F32) == rank
            low_value = jnp.where(group < 2, lanes[2 + k:3 + k, cols], (number & 255).astype(F32))
            high_value = jnp.where(group < 2, lanes[4 + k:5 + k, cols], ((number >> 8) + 4 * k).astype(F32))
            low16 = jnp.where(same, low_value, 0.0).astype(BF16)
            high16 = jnp.where(same, high_value, 0.0).astype(BF16)
            meta_low = meta_low + lax.dot_general(hit16, low16, NT, preferred_element_type=F32)
            meta_high = meta_high + lax.dot_general(hit16, high16, NT, preferred_element_type=F32)
    meta = meta_low + 256.0 * meta_high
    for t in range(16):
        for d in range(8):
            meta0[t, d] = meta[t * 8 + d:t * 8 + d + 1, :]
    slot_id = iota((32, MINE), 0).astype(F32)
    for k in range(2):
        mask_ref[k] = jnp.where(slot_id == rank_ref[k:k + 1, :], 1.0, 0.0).astype(BF16)

    meta1[0] = meta0[tile]

    def small_meta(u, carry):
        t = jnp.bitwise_xor(tile, u)
        remote(meta0.at[t], meta1.at[u], pair(m1_sem), dom, t).start()
        return carry

    lax.fori_loop(1, 16, small_meta, 0)

    def turn_of(i):
        return lax.rem(7 * (i + 1), 16)

    def pack(i, carry):
        blocks = []
        for e in range(8):
            t = jnp.bitwise_xor(tile, jnp.bitwise_xor(turn_of(i), SHIFT[e]))
            d = pl.ds(jnp.bitwise_xor(dom, e), 1)
            one = ot[0, t, d, :].astype(BF16)
            two = ot[1, t, d, :].astype(BF16)
            blocks.append(mask_ref[0] * one + mask_ref[1] * two)
        rows = jnp.dot(jnp.concatenate(blocks, axis=0), wi[...], preferred_element_type=F32).astype(BF16)
        for e in range(8):
            sb[i, e] = rows[e * 32:(e + 1) * 32]
        return carry

    pl.semaphore_wait(all_sem, 7)

    def ship(i, carry):
        for e in range(8):
            t = jnp.bitwise_xor(tile, jnp.bitwise_xor(turn_of(i), SHIFT[e]))
            d = jnp.bitwise_xor(dom, e)
            remote(sb.at[i, e], rb.at[i, e], (data_send, data_recv.at[i]), d, t).start()
        return carry

    def pack_ship(i, carry):
        pack(i, 0)
        return ship(i, 0)

    lax.fori_loop(0, FIRST, pack_ship, 0)

    wait_for(meta1.at[pl.ds(1, 15)], m1_sem.at[1])
    for u in range(16):
        meta2[0, u] = meta1[u, dom]

    def forward(e, carry):
        d = jnp.bitwise_xor(dom, e)
        remote(meta1.at[:, d], meta2.at[e], pair(m2_sem), d, tile).start()
        return carry

    lax.fori_loop(1, 8, forward, 0)

    wait_for(xw.at[other], xw_sem.at[1])
    row = tile // 4
    column = lax.rem(tile, 4)
    for c in range(REFS // CHUNK):
        loads(c).wait()

    def scored(i, carry):
        chunk = jnp.bitwise_xor(row, lax.rem(i + 1, 4))
        base = pl.multiple_of(chunk * CHUNK, CHUNK)

        def block(b, inner):
            refs = rv[pl.ds(base + b * 16, 16)].reshape(256, 256)
            turned = jnp.dot(swap, refs, preferred_element_type=F32)
            squares = (turned[:, :HALF] * turned[:, :HALF] + turned[:, HALF:] * turned[:, HALF:]).astype(BF16)
            turned = turned.astype(BF16)
            at = pl.multiple_of(b * 16, 16)
            for r in range(16):
                xc[pl.ds(at, 16), r * WIDE:r * WIDE + 256] = turned[r * 16:(r + 1) * 16]
                xc[pl.ds(at, 16), r * WIDE + 256:(r + 1) * WIDE] = squares[r * 16:(r + 1) * 16]
            return inner

        lax.fori_loop(0, CHUNK // 16, block, 0, unroll=8)
        score[pl.ds(base, CHUNK), :] = SCALE * lax.dot_general(xc[...], xw[...], NT, preferred_element_type=F32)

        def share(v, inner):
            t = chunk * 4 + jnp.bitwise_xor(column, v)
            u = jnp.bitwise_xor(t, tile)

            @pl.when(u != 0)
            def _():
                remote(score.at[pl.ds(pl.multiple_of(t * 64, 64), 64)], part.at[u], pair(part_sem), dom, t).start()

            return inner

        lax.fori_loop(0, 4, share, 0)
        return carry

    lax.fori_loop(0, 4, scored, 0)
    part[0] = score[pl.ds(pl.multiple_of(tile * 64, 64), 64), :]
    lax.fori_loop(FIRST, SECOND, pack_ship, 0)

    wait_for(info.at[pl.ds(1, 7)], info_sem.at[1])
    wait_for(noise.at[pl.ds(1, 15)], noise_sem.at[1])
    wait_for(meta2.at[pl.ds(1, 7)], m2_sem.at[1])
    lane1 = iota((1, HALF), 1)
    stack[...] = jnp.zeros_like(stack)
    for w in range(4):
        focus = jnp.where(lane1 < PD, info[2 * w, 2:3, :], info[2 * w + 1, 2:3, :])
        first = focus.astype(BF16).astype(F32)
        second = (focus - first).astype(BF16).astype(F32)
        stack[4 * w:4 * w + 1, :] = first
        stack[4 * w + 1:4 * w + 2, :] = second
        stack[4 * w + 2:4 * w + 3, :] = focus - first - second
    focus_rows = stack[...].astype(BF16)
    lane2 = iota((1, 256), 1)

    def prepare(i, carry):
        u = turn_of(i)
        quarter = lane1 >> 5
        strips, numbers = [], []
        for half in range(2):
            strip = jnp.zeros((1, HALF), F32)
            number = jnp.zeros((1, HALF), F32)
            for a in range(4):
                e = half * 4 + a
                got = meta2[e, jnp.bitwise_xor(u, SHIFT[e])]
                back = pltpu.roll(got, 64, 1)
                strip = jnp.where(quarter == a, got if a < 2 else back, strip)
                number = jnp.where(quarter == a, back if a < 2 else got, number)
            strips.append(strip)
            numbers.append(number)
        strip = jnp.concatenate(strips, axis=1).astype(I32) - 1
        number = jnp.concatenate(numbers, axis=1).astype(I32)
        low[i] = (strip & 255).astype(F32)
        high[i] = (strip >> 8).astype(F32)
        r = number & 15
        particle = ((number >> 4) & 63) + 64 * ((lane2 >> 5) & 1)
        code[i] = (particle + 128 * (number >> 10)).astype(F32)
        hot = jnp.where(iota((HALF, 256), 0) == particle, 1.0, 0.0).astype(BF16)
        found = jnp.dot(focus_rows, hot, preferred_element_type=F32)
        found = jnp.where((iota((16, 256), 0) >> 2) == (lane2 >> 6), found, 0.0)
        slope = jnp.sum(found, axis=0, keepdims=True) * TURN
        source = lane2 >> 5
        shift = ((source & 1) * 5) ^ (((source >> 1) & 1) * 10) ^ ((source >> 2) * 3)
        row_f = freq_sq((shift ^ jnp.bitwise_xor(tile, u)) * 16 + r)
        offset = slope * (row_f * row_f) + PHASE
        which = iota((8, 256), 0)
        rows = jnp.where(which == 0, slope, jnp.where(which == 1, offset, jnp.where(which == 2, (r + 16 * source).astype(F32), strip.astype(F32))))
        turned = jnp.transpose(rows)
        col_f = iota((256, HALF), 1).astype(F32)
        contrast = wave(turned[:, 0:1] * (col_f * col_f) + turned[:, 1:2])
        pick_row = jnp.where(iota((256, HALF), 1).astype(F32) == turned[:, 2:3], 1.0, 0.0).astype(BF16)
        pick_row = jnp.concatenate([pick_row] * 3, axis=1)
        full = jnp.concatenate([noise[jnp.bitwise_xor(u, SHIFT[e])] for e in range(8)], axis=0)
        first = full.astype(BF16)
        second = (full - first.astype(F32)).astype(BF16)
        third = (full - first.astype(F32) - second.astype(F32)).astype(BF16)
        gain = jnp.dot(pick_row, jnp.concatenate([first, second, third], axis=0), preferred_element_type=F32)
        power = contrast * contrast * gain
        upper_half = turned[:, 3:4] >= 1024.0
        pm[i, :, 0:HALF] = jnp.where(upper_half, 0.0, power).astype(BF16)
        pm[i, :, HALF:] = jnp.where(upper_half, power, 0.0).astype(BF16)
        return carry

    lax.fori_loop(0, 8, prepare, 0)

    wait_for(part.at[pl.ds(1, 15)], part_sem.at[1])
    total = part[0]
    for u in range(1, 16):
        total = total + part[u]
    same_core = jnp.where(core == 0, 0, 1)
    cand = []
    for k in range(2):
        zero = info[same_core, k:k + 1, :]
        one = info[1 - same_core, k:k + 1, :]
        cand.append(jnp.where(lane1 < PD, zero, one))
    ids = (iota((64, HALF), 0) + core * REFS + tile * 64).astype(F32)
    top = jnp.max(total, axis=0, keepdims=True)
    mass = jnp.sum(jnp.exp(total - top), axis=0, keepdims=True)
    got0 = jnp.sum(jnp.where(ids == cand[0], total, 0.0), axis=0, keepdims=True)
    got1 = jnp.sum(jnp.where(ids == cand[1], total, 0.0), axis=0, keepdims=True)
    which = iota((8, HALF), 0)
    stats[0] = jnp.where(which == 0, top, jnp.where(which == 1, mass, jnp.where(which == 2, got0, got1)))

    def tell(v, carry):
        d = jnp.bitwise_xor(dom, v // 16)
        t = jnp.bitwise_xor(tile, lax.rem(v, 16))
        remote(stats.at[0], stats.at[v], pair(stat_sem), d, t).start()
        return carry

    lax.fori_loop(1, 32, tell, 0)
    lax.fori_loop(SECOND, THIRD, pack_ship, 0)
    lax.fori_loop(8, 12, prepare, 0)
    wait_for(stats.at[pl.ds(1, 31)], stat_sem.at[1])
    every = stats[...]
    tops = every[:, 0, :]
    top = jnp.max(tops, axis=0, keepdims=True)
    mass = jnp.sum(every[:, 1, :] * jnp.exp(tops - top), axis=0, keepdims=True)
    got0 = jnp.sum(every[:, 2, :], axis=0, keepdims=True)
    got1 = jnp.sum(every[:, 3, :], axis=0, keepdims=True)
    spread = jnp.log(mass)
    best = jnp.maximum(got0, got1)
    raised0 = jnp.exp(got0 - best)
    raised1 = jnp.exp(got1 - best)
    chosen0 = raised0 / (raised0 + raised1)
    chosen1 = raised1 / (raised0 + raised1)
    rows = jnp.where(which == 0, chosen0, jnp.where(which == 1, chosen1, spread))
    rows = jnp.where(core == 0, rows, pltpu.roll(rows, 64, 1))
    picks[0] = rows
    spread_ref[...] = rows

    def pass_on(w, carry):
        remote(picks.at[0], picks.at[w], pair(pick_sem), jnp.bitwise_xor(dom, 2 * w), tile).start()
        return carry

    lax.fori_loop(1, 4, pass_on, 0)
    lax.fori_loop(THIRD, 15, pack_ship, 0)
    pack(15, 0)
    rb[15, 0] = sb[15, 0]

    for e in range(1, 8):
        t = jnp.bitwise_xor(tile, SHIFT[e])
        remote(sb.at[15, e], rb.at[15, e], (data_send, data_recv.at[15]), jnp.bitwise_xor(dom, e), t).start()
    lax.fori_loop(12, 16, prepare, 0)
    wait_for(picks.at[pl.ds(1, 3)], pick_sem.at[1])
    for w in range(4):
        table[2 * w:2 * w + 2, :] = picks[w, 0:2, :]
    chosen_rows = table[...].astype(BF16)

    def choose(u, carry):
        number = code[u].astype(I32)
        hot = jnp.where(iota((HALF, 256), 0) == (number & 127), 1.0, 0.0).astype(BF16)
        found = jnp.dot(chosen_rows, hot, preferred_element_type=F32)
        keep = iota((8, 256), 0) == ((lane2 >> 6) * 2 + (number >> 7))
        weight[u] = jnp.sum(jnp.where(keep, found, 0.0), axis=0, keepdims=True)
        return carry

    lax.fori_loop(0, 16, choose, 0, unroll=8)

    slab_row = iota((256, 4 * 256), 0).astype(F32).astype(BF16)
    for g in range(4):
        for i in range(4 * g, 4 * g + 4):
            if i == 15:
                wait_for(rb.at[15, pl.ds(1, 7)], data_recv.at[15])
            else:
                wait_for(rb.at[i], data_recv.at[i])
        low_row = jnp.concatenate([low[i] for i in range(4 * g, 4 * g + 4)], axis=1)
        high_row = jnp.concatenate([high[i] for i in range(4 * g, 4 * g + 4)], axis=1)
        share_row = jnp.concatenate([weight[i] for i in range(4 * g, 4 * g + 4)], axis=1)
        if g == 3:
            rows_ref[...] = rb[12:16].reshape(1024, 256)
            power_ref[...] = pm[12:16].reshape(1024, 256)
            label_ref[0:1, :] = low_row
            label_ref[1:2, :] = high_row
            label_ref[2:3, :] = share_row
            break
        low16 = low_row.astype(BF16)

        def insert(b, carry):
            match = slab_row == low16
            rows = rb[4 * g:4 * g + 4].reshape(1024, 256)
            power = pm[4 * g:4 * g + 4].reshape(1024, 256)
            spots = []
            for h in range(2):
                value = jnp.where(high_row == (b + 4 * h).astype(F32), share_row, 0.0).astype(BF16)
                spots.append(jnp.where(match, value, jnp.zeros_like(value)))
            both = jnp.dot(spots[0] + spots[1], power, preferred_element_type=F32)
            for h in range(2):
                at = pl.ds(pl.multiple_of((b + 4 * h) * 256, 256), 256)
                data = jnp.dot(spots[h], rows, preferred_element_type=F32)
                more = both[:, h * HALF:(h + 1) * HALF]
                if g == 0:
                    vol_ref[at, 0:256] = data
                    vol_ref[at, 256:] = more
                else:
                    vol_ref[at, 0:256] += data
                    vol_ref[at, 256:] += more
            return carry

        lax.fori_loop(0, 4, insert, 0)

    wait_for(xw.at[mine], xw_sem.at[0])
    wait_for(meta1.at[pl.ds(1, 15)], m1_sem.at[0])
    wait_for(noise.at[pl.ds(1, 15)], noise_sem.at[0])
    wait_for(info.at[pl.ds(1, 7)], info_sem.at[0])
    wait_for(meta2.at[pl.ds(1, 7)], m2_sem.at[0])
    wait_for(part.at[pl.ds(1, 15)], part_sem.at[0])
    wait_for(stats.at[pl.ds(1, 31)], stat_sem.at[0])
    wait_for(picks.at[pl.ds(1, 3)], pick_sem.at[0])
    wait_for(sb.at[pl.ds(0, 15)], data_send)
    wait_for(sb.at[15, pl.ds(1, 7)], data_send)


def finish(part_ref, rows_ref, power_ref, label_ref, stat_ref, vol_ref, spread_ref):
    b = pl.program_id(0)
    match = iota((256, 1024), 0).astype(F32).astype(BF16) == label_ref[0:1, :].astype(BF16)
    spots = []
    for h in range(2):
        value = jnp.where(label_ref[1:2, :] == (b + 4 * h).astype(F32), label_ref[2:3, :], 0.0).astype(BF16)
        spots.append(jnp.where(match, value, jnp.zeros_like(value)))
    both = jnp.dot(spots[0] + spots[1], power_ref[...], preferred_element_type=F32)
    for h in range(2):
        data = jnp.dot(spots[h], rows_ref[...], preferred_element_type=F32)
        vol_ref[h, :, 0:256] = part_ref[h, :, 0:256] + data
        vol_ref[h, :, 256:] = part_ref[h, :, 256:] + both[:, h * HALF:(h + 1) * HALF]
    spread_ref[...] = stat_ref[2:3, 0:PD]


def shards(images, defocus, noise_weight, references, candidates, route, strips):
    rows = images.reshape(MINE, 2 * HALF)
    focus = defocus[None]
    turned = [jnp.transpose(x[0, 0], (1, 2, 0)) for x in (route, strips)]
    vmem = pl.BlockSpec(memory_space=pltpu.VMEM)
    dma = pltpu.SemaphoreType.DMA
    partial, last_rows, last_power, labels, stat = pl.pallas_call(
        kernel,
        out_shape=(
            jax.ShapeDtypeStruct((STRIPS, WIDE), F32),
            jax.ShapeDtypeStruct((1024, 256), BF16),
            jax.ShapeDtypeStruct((1024, 256), BF16),
            jax.ShapeDtypeStruct((8, 1024), F32),
            jax.ShapeDtypeStruct((8, HALF), F32),
        ),
        in_specs=[vmem, vmem, vmem, vmem, pl.BlockSpec(memory_space=pl.ANY), vmem, vmem],
        out_specs=(vmem,) * 5,
        scratch_shapes=[
            pltpu.VMEM((REFS, ROWS_DEV, 2 * HALF), BF16),
            pltpu.VMEM((CHUNK, DEPTH), BF16),
            pltpu.VMEM((2 * PD, DEPTH), BF16),
            pltpu.VMEM((MINE, 2 * HALF), BF16),
            pltpu.VMEM((MINE, HALF), BF16),
            pltpu.VMEM((2, 16, 8, MINE), F32),
            pltpu.VMEM((2, MINE), F32),
            pltpu.VMEM((2, 32, MINE), BF16),
            pltpu.VMEM((16, 8, 32, 256), BF16),
            pltpu.VMEM((16, 8, 32, 256), BF16),
            pltpu.VMEM((16, 8, 1, HALF), F32),
            pltpu.VMEM((16, 8, 1, HALF), F32),
            pltpu.VMEM((8, 16, 1, HALF), F32),
            pltpu.VMEM((8, MINE), F32),
            pltpu.VMEM((8, 8, HALF), F32),
            pltpu.VMEM((16, 16, HALF), F32),
            pltpu.VMEM((REFS, 2 * PD), F32),
            pltpu.VMEM((16, 64, 2 * PD), F32),
            pltpu.VMEM((32, 8, HALF), F32),
            pltpu.VMEM((4, 8, HALF), F32),
            pltpu.VMEM((16, HALF), F32),
            pltpu.VMEM((8, HALF), F32),
            pltpu.VMEM((16, 1, 256), F32),
            pltpu.VMEM((16, 1, 256), F32),
            pltpu.VMEM((16, 1, 256), F32),
            pltpu.VMEM((16, 1, 256), F32),
            pltpu.VMEM((16, 256, 256), BF16),
            dma((REFS // CHUNK,)),
            dma,
            dma((16,)),
            pltpu.SemaphoreType.REGULAR,
        ] + [dma((2,))] * 8,
        compiler_params=pltpu.CompilerParams(
            collective_id=0, has_side_effects=True, vmem_limit_bytes=56 << 20
        ),
    )(rows, focus, candidates.T, noise_weight, references, *turned)
    half = pl.BlockSpec((2, 256, WIDE), lambda b: (0, b, 0))

    def whole(shape):
        return pl.BlockSpec(shape, lambda b: (0, 0))

    volume, spread = pl.pallas_call(
        finish,
        grid=(4,),
        out_shape=(
            jax.ShapeDtypeStruct((2, STRIPS // 2, WIDE), F32),
            jax.ShapeDtypeStruct((1, PD), F32),
        ),
        in_specs=[half, whole((1024, 256)), whole((1024, 256)), whole((8, 1024)), whole((8, HALF))],
        out_specs=(half, whole((1, PD))),
        compiler_params=pltpu.CompilerParams(vmem_limit_bytes=62 << 20),
    )(partial.reshape(2, STRIPS // 2, WIDE), last_rows, last_power, labels, stat)
    return volume.reshape(STRIPS, WIDE), spread[0]


def solution(mesh):
    in_specs = (
        P("dom", "tile", None),
        P("dom"),
        P("tile", None),
        P(None, "tile", None),
        P("dom", None),
        P("dom", "tile", None, None, None),
        P("dom", "tile", None, None, None),
    )
    out_specs = (P(("dom", "tile"), None), P("dom"))
    return jax.shard_map(shards, mesh=mesh, in_specs=in_specs, out_specs=out_specs, check_vma=False)
```

```python
import math

import jax
import jax.numpy as jnp
from jax import lax
from jax.experimental import pallas as pl
from jax.experimental.pallas import tpu as pltpu
from jax.sharding import PartitionSpec as P

F32 = jnp.float32
BF16 = jnp.bfloat16
I32 = jnp.int32
MESH = pl.DeviceIdType.MESH
NT = (((1,), (1,)), ((), ()))

STRIPS = 2048
HALF = 128
ROWS_DEV = 16
PD = 64
MINE = PD * ROWS_DEV
NREF = 2048
REFS = NREF // 2
WIDE = 3 * HALF
DEPTH = ROWS_DEV * WIDE
CHUNK = 256
FIRST, SECOND, THIRD = 6, 8, 11
SHIFT = (0, 5, 10, 15, 3, 6, 9, 12)

TURN = 400.0 / 65536.0 / (2.0 * math.pi)
PHASE = 0.1 / (2.0 * math.pi)
SCALE = 1.0 / math.sqrt(32768.0)
SERIES = (
    6.283182793407029,
    -41.34141938561706,
    81.59613875538182,
    -76.5796878510169,
    41.20374363365668,
    -12.268859941003917,
)


def wave(turns):
    frac = turns - jnp.floor(turns + 0.5)
    sq = frac * frac
    total = jnp.full_like(sq, SERIES[-1])
    for coef in SERIES[-2::-1]:
        total = total * sq + coef
    return total * frac


def iota(shape, dim):
    return lax.broadcasted_iota(I32, shape, dim)


def kernel(
    img_ref, focus_ref, cand_ref, noise_ref, refs_ref, route_ref, place_ref,
    vol_ref, rows_ref, power_ref, label_ref, spread_ref,
    rv, xc, xw, wi, pmo, ot, rank_ref, mask_ref, sb, rb, meta0, meta1, meta2,
    lanes, info, noise, score, part, stats, picks, stack, table, low, high, code, weight, pm,
    ref_sem, data_send, data_recv, all_sem, xw_sem, info_sem, noise_sem, m1_sem, m2_sem, part_sem, stat_sem, pick_sem,
):
    dom = lax.axis_index("dom")
    tile = lax.axis_index("tile")
    core = lax.rem(dom, 2)
    barrier = pltpu.get_barrier_semaphore()

    def loads(c):
        return pltpu.make_async_copy(
            refs_ref.at[pl.ds(core * REFS + c * CHUNK, CHUNK)],
            rv.at[pl.ds(c * CHUNK, CHUNK)],
            ref_sem.at[c],
        )

    for c in range(REFS // CHUNK):
        loads(c).start()

    def greet_tile(u, carry):
        pl.semaphore_signal(barrier, inc=1, device_id=(dom, jnp.bitwise_xor(tile, u)), device_id_type=MESH)
        return carry

    def greet_dom(e, carry):
        pl.semaphore_signal(barrier, inc=1, device_id=(jnp.bitwise_xor(dom, e), tile), device_id_type=MESH)
        return carry

    def vouch(e, carry):
        pl.semaphore_signal(all_sem, inc=1, device_id=(jnp.bitwise_xor(dom, e), tile), device_id_type=MESH)
        return carry

    lax.fori_loop(1, 16, greet_tile, 0)
    lax.fori_loop(1, 8, greet_dom, 0)

    def remote(src, dst, sems, d, t):
        return pltpu.make_async_remote_copy(
            src_ref=src, dst_ref=dst, send_sem=sems[0], recv_sem=sems[1],
            device_id=(d, t), device_id_type=MESH,
        )

    def pair(sem):
        return sem.at[0], sem.at[1]

    def wait_for(ref, sem):
        pltpu.make_async_copy(ref, ref, sem).wait()

    info[0] = jnp.zeros((8, HALF), F32)
    for k in range(2):
        cand_row = cand_ref[k:k + 1, :].astype(F32)
        info[0, k:k + 1, :] = jnp.concatenate([cand_row, cand_row], axis=1)
    info[0, 2:3, :] = jnp.concatenate([focus_ref[...], focus_ref[...]], axis=1)
    widen = jnp.where((iota((PD, MINE), 1) >> 4) == iota((PD, MINE), 0), 1.0, 0.0).astype(BF16)
    diagonal = (iota((16, MINE), 1) & 15) == iota((16, MINE), 0)

    def along(block):
        wide = jnp.dot(block.astype(F32).astype(BF16), widen, preferred_element_type=F32)
        return jnp.sum(jnp.where(diagonal, wide, 0.0), axis=0, keepdims=True)

    for k in range(2):
        lanes[k:k + 1, :] = along(route_ref[k])
        place = place_ref[k] + 1
        lanes[2 + k:3 + k, :] = along(place & 255)
        lanes[4 + k:5 + k, :] = along(place >> 8)

    def freq_sq(rows):
        return jnp.where(rows < 128, rows, rows - 256).astype(F32)

    focus_row = info[0, 2:3, :]

    def weigh(c, carry):
        row = iota((128, HALF), 0)
        lane = iota((128, HALF), 1)
        row_f = freq_sq(tile * 16 + (row & 15))
        col_f = lane.astype(F32)
        radius = row_f * row_f + col_f * col_f
        focus = jnp.sum(jnp.where(lane == c * 8 + (row >> 4), focus_row, 0.0), axis=1, keepdims=True)
        contrast = -wave(focus * TURN * radius + PHASE)
        noise_here = jnp.concatenate([noise_ref[...]] * 8, axis=0)
        start = pl.multiple_of(c * 128, 128)
        pmo[pl.ds(start, 128), :] = (contrast * contrast * noise_here).astype(BF16)
        gain = contrast * noise_here
        rows = img_ref[pl.ds(start, 128), :].astype(F32)
        wi[pl.ds(start, 128), 0:HALF] = (gain * rows[:, :HALF]).astype(BF16)
        wi[pl.ds(start, 128), HALF:] = (gain * rows[:, HALF:]).astype(BF16)
        return carry

    lax.fori_loop(0, 8, weigh, 0)

    ia, ib = iota((256, 256), 0), iota((256, 256), 1)
    swap = jnp.where(((ia & 15) * 16 + (ia >> 4)) == ib, 1.0, 0.0).astype(BF16)
    for b in range(4):
        at = pl.multiple_of(core * PD + b * 16, 16)
        left = jnp.dot(swap, wi[b * 256:(b + 1) * 256, :], preferred_element_type=F32).astype(BF16)
        right = (-0.5 * jnp.dot(swap, pmo[b * 256:(b + 1) * 256, :], preferred_element_type=F32)).astype(BF16)
        for i in range(16):
            xw[pl.ds(at, 16), i * WIDE:i * WIDE + 256] = left[i * 16:(i + 1) * 16]
            xw[pl.ds(at, 16), i * WIDE + 256:(i + 1) * WIDE] = right[i * 16:(i + 1) * 16]

    pl.semaphore_wait(barrier, 22)
    lax.fori_loop(1, 8, vouch, 0)
    mate = jnp.bitwise_xor(dom, 1)
    mine = pl.ds(pl.multiple_of(core * PD, PD), PD)
    other = pl.ds(pl.multiple_of((1 - core) * PD, PD), PD)
    remote(xw.at[mine], xw.at[mine], pair(xw_sem), mate, tile).start()
    noise[0] = noise_ref[...]

    def small(u, carry):
        t = jnp.bitwise_xor(tile, u)
        remote(noise_ref, noise.at[u], pair(noise_sem), dom, t).start()
        return carry

    lax.fori_loop(1, 16, small, 0)

    def small_dom(e, carry):
        remote(info.at[0], info.at[e], pair(info_sem), jnp.bitwise_xor(dom, e), tile).start()
        return carry

    lax.fori_loop(1, 8, small_dom, 0)

    upper = jnp.where(ia < ib, 1.0, 0.0).astype(BF16)
    running = jnp.zeros((128, 1), F32)
    meta_low = jnp.zeros((128, 128), F32)
    meta_high = jnp.zeros((128, 128), F32)
    owner_id = iota((128, 256), 0)
    for k in range(2):
        for b in range(4):
            cols = slice(b * 256, (b + 1) * 256)
            owner = lanes[k:k + 1, cols].astype(I32)
            owner = ((owner & 15) << 3) | (owner >> 4)
            hit = jnp.where(owner_id == owner, 1.0, 0.0)
            hit16 = hit.astype(BF16)
            before = jnp.dot(hit16, upper, preferred_element_type=F32) + running
            rank = jnp.sum(hit * before, axis=0, keepdims=True)
            running = running + jnp.sum(hit, axis=1, keepdims=True)
            for t in range(16):
                ot[k, t, :, cols] = hit[t * 8:(t + 1) * 8]
            rank_ref[k:k + 1, cols] = rank
            number = iota((1, 256), 1) + b * 256
            group = owner_id >> 5
            same = (owner_id & 31).astype(F32) == rank
            low_value = jnp.where(group < 2, lanes[2 + k:3 + k, cols], (number & 255).astype(F32))
            high_value = jnp.where(group < 2, lanes[4 + k:5 + k, cols], ((number >> 8) + 4 * k).astype(F32))
            low16 = jnp.where(same, low_value, 0.0).astype(BF16)
            high16 = jnp.where(same, high_value, 0.0).astype(BF16)
            meta_low = meta_low + lax.dot_general(hit16, low16, NT, preferred_element_type=F32)
            meta_high = meta_high + lax.dot_general(hit16, high16, NT, preferred_element_type=F32)
    meta = meta_low + 256.0 * meta_high
    for t in range(16):
        for d in range(8):
            meta0[t, d] = meta[t * 8 + d:t * 8 + d + 1, :]
    slot_id = iota((32, MINE), 0).astype(F32)
    for k in range(2):
        mask_ref[k] = jnp.where(slot_id == rank_ref[k:k + 1, :], 1.0, 0.0).astype(BF16)

    meta1[0] = meta0[tile]

    def small_meta(u, carry):
        t = jnp.bitwise_xor(tile, u)
        remote(meta0.at[t], meta1.at[u], pair(m1_sem), dom, t).start()
        return carry

    lax.fori_loop(1, 16, small_meta, 0)

    def turn_of(i):
        return lax.rem(7 * (i + 1), 16)

    def pack(i, carry):
        blocks = []
        for e in range(8):
            t = jnp.bitwise_xor(tile, jnp.bitwise_xor(turn_of(i), SHIFT[e]))
            d = pl.ds(jnp.bitwise_xor(dom, e), 1)
            one = ot[0, t, d, :].astype(BF16)
            two = ot[1, t, d, :].astype(BF16)
            blocks.append(mask_ref[0] * one + mask_ref[1] * two)
        rows = jnp.dot(jnp.concatenate(blocks, axis=0), wi[...], preferred_element_type=F32).astype(BF16)
        for e in range(8):
            sb[i, e] = rows[e * 32:(e + 1) * 32]
        return carry

    pl.semaphore_wait(all_sem, 7)

    def ship(i, carry):
        for e in range(8):
            t = jnp.bitwise_xor(tile, jnp.bitwise_xor(turn_of(i), SHIFT[e]))
            d = jnp.bitwise_xor(dom, e)
            remote(sb.at[i, e], rb.at[i, e], (data_send, data_recv.at[i]), d, t).start()
        return carry

    def pack_ship(i, carry):
        pack(i, 0)
        return ship(i, 0)

    lax.fori_loop(0, FIRST, pack_ship, 0)

    wait_for(meta1.at[pl.ds(1, 15)], m1_sem.at[1])
    for u in range(16):
        meta2[0, u] = meta1[u, dom]

    def forward(e, carry):
        d = jnp.bitwise_xor(dom, e)
        remote(meta1.at[:, d], meta2.at[e], pair(m2_sem), d, tile).start()
        return carry

    lax.fori_loop(1, 8, forward, 0)

    wait_for(xw.at[other], xw_sem.at[1])
    row = tile // 4
    column = lax.rem(tile, 4)
    for c in range(REFS // CHUNK):
        loads(c).wait()

    def scored(i, carry):
        chunk = jnp.bitwise_xor(row, lax.rem(i + 1, 4))
        base = pl.multiple_of(chunk * CHUNK, CHUNK)

        def block(b, inner):
            refs = rv[pl.ds(base + b * 16, 16)].reshape(256, 256)
            turned = jnp.dot(swap, refs, preferred_element_type=F32)
            squares = (turned[:, :HALF] * turned[:, :HALF] + turned[:, HALF:] * turned[:, HALF:]).astype(BF16)
            turned = turned.astype(BF16)
            at = pl.multiple_of(b * 16, 16)
            for r in range(16):
                xc[pl.ds(at, 16), r * WIDE:r * WIDE + 256] = turned[r * 16:(r + 1) * 16]
                xc[pl.ds(at, 16), r * WIDE + 256:(r + 1) * WIDE] = squares[r * 16:(r + 1) * 16]
            return inner

        lax.fori_loop(0, CHUNK // 16, block, 0, unroll=8)
        score[pl.ds(base, CHUNK), :] = SCALE * lax.dot_general(xc[...], xw[...], NT, preferred_element_type=F32)

        def share(v, inner):
            t = chunk * 4 + jnp.bitwise_xor(column, v)
            u = jnp.bitwise_xor(t, tile)

            @pl.when(u != 0)
            def _():
                remote(score.at[pl.ds(pl.multiple_of(t * 64, 64), 64)], part.at[u], pair(part_sem), dom, t).start()

            return inner

        lax.fori_loop(0, 4, share, 0)
        return carry

    lax.fori_loop(0, 4, scored, 0)
    part[0] = score[pl.ds(pl.multiple_of(tile * 64, 64), 64), :]
    lax.fori_loop(FIRST, SECOND, pack_ship, 0)

    wait_for(info.at[pl.ds(1, 7)], info_sem.at[1])
    wait_for(noise.at[pl.ds(1, 15)], noise_sem.at[1])
    wait_for(meta2.at[pl.ds(1, 7)], m2_sem.at[1])
    lane1 = iota((1, HALF), 1)
    stack[...] = jnp.zeros_like(stack)
    for w in range(4):
        focus = jnp.where(lane1 < PD, info[2 * w, 2:3, :], info[2 * w + 1, 2:3, :])
        first = focus.astype(BF16).astype(F32)
        second = (focus - first).astype(BF16).astype(F32)
        stack[4 * w:4 * w + 1, :] = first
        stack[4 * w + 1:4 * w + 2, :] = second
        stack[4 * w + 2:4 * w + 3, :] = focus - first - second
    focus_rows = stack[...].astype(BF16)
    lane2 = iota((1, 256), 1)

    def prepare(i, carry):
        u = turn_of(i)
        quarter = lane1 >> 5
        strips, numbers = [], []
        for half in range(2):
            strip = jnp.zeros((1, HALF), F32)
            number = jnp.zeros((1, HALF), F32)
            for a in range(4):
                e = half * 4 + a
                got = meta2[e, jnp.bitwise_xor(u, SHIFT[e])]
                back = pltpu.roll(got, 64, 1)
                strip = jnp.where(quarter == a, got if a < 2 else back, strip)
                number = jnp.where(quarter == a, back if a < 2 else got, number)
            strips.append(strip)
            numbers.append(number)
        strip = jnp.concatenate(strips, axis=1).astype(I32) - 1
        number = jnp.concatenate(numbers, axis=1).astype(I32)
        low[i] = (strip & 255).astype(F32)
        high[i] = (strip >> 8).astype(F32)
        r = number & 15
        particle = ((number >> 4) & 63) + 64 * ((lane2 >> 5) & 1)
        code[i] = (particle + 128 * (number >> 10)).astype(F32)
        hot = jnp.where(iota((HALF, 256), 0) == particle, 1.0, 0.0).astype(BF16)
        found = jnp.dot(focus_rows, hot, preferred_element_type=F32)
        found = jnp.where((iota((16, 256), 0) >> 2) == (lane2 >> 6), found, 0.0)
        slope = jnp.sum(found, axis=0, keepdims=True) * TURN
        source = lane2 >> 5
        shift = ((source & 1) * 5) ^ (((source >> 1) & 1) * 10) ^ ((source >> 2) * 3)
        row_f = freq_sq((shift ^ jnp.bitwise_xor(tile, u)) * 16 + r)
        offset = slope * (row_f * row_f) + PHASE
        which = iota((8, 256), 0)
        rows = jnp.where(which == 0, slope, jnp.where(which == 1, offset, jnp.where(which == 2, (r + 16 * source).astype(F32), strip.astype(F32))))
        turned = jnp.transpose(rows)
        col_f = iota((256, HALF), 1).astype(F32)
        contrast = wave(turned[:, 0:1] * (col_f * col_f) + turned[:, 1:2])
        pick_row = jnp.where(iota((256, HALF), 1).astype(F32) == turned[:, 2:3], 1.0, 0.0).astype(BF16)
        pick_row = jnp.concatenate([pick_row] * 3, axis=1)
        full = jnp.concatenate([noise[jnp.bitwise_xor(u, SHIFT[e])] for e in range(8)], axis=0)
        first = full.astype(BF16)
        second = (full - first.astype(F32)).astype(BF16)
        third = (full - first.astype(F32) - second.astype(F32)).astype(BF16)
        gain = jnp.dot(pick_row, jnp.concatenate([first, second, third], axis=0), preferred_element_type=F32)
        power = contrast * contrast * gain
        upper_half = turned[:, 3:4] >= 1024.0
        pm[i, :, 0:HALF] = jnp.where(upper_half, 0.0, power).astype(BF16)
        pm[i, :, HALF:] = jnp.where(upper_half, power, 0.0).astype(BF16)
        return carry

    lax.fori_loop(0, 8, prepare, 0)

    wait_for(part.at[pl.ds(1, 15)], part_sem.at[1])
    total = part[0]
    for u in range(1, 16):
        total = total + part[u]
    same_core = jnp.where(core == 0, 0, 1)
    cand = []
    for k in range(2):
        zero = info[same_core, k:k + 1, :]
        one = info[1 - same_core, k:k + 1, :]
        cand.append(jnp.where(lane1 < PD, zero, one))
    ids = (iota((64, HALF), 0) + core * REFS + tile * 64).astype(F32)
    top = jnp.max(total, axis=0, keepdims=True)
    mass = jnp.sum(jnp.exp(total - top), axis=0, keepdims=True)
    got0 = jnp.sum(jnp.where(ids == cand[0], total, 0.0), axis=0, keepdims=True)
    got1 = jnp.sum(jnp.where(ids == cand[1], total, 0.0), axis=0, keepdims=True)
    which = iota((8, HALF), 0)
    stats[0] = jnp.where(which == 0, top, jnp.where(which == 1, mass, jnp.where(which == 2, got0, got1)))

    def tell(v, carry):
        d = jnp.bitwise_xor(dom, v // 16)
        t = jnp.bitwise_xor(tile, lax.rem(v, 16))
        remote(stats.at[0], stats.at[v], pair(stat_sem), d, t).start()
        return carry

    lax.fori_loop(1, 32, tell, 0, unroll=True)
    lax.fori_loop(SECOND, THIRD, pack_ship, 0)
    lax.fori_loop(8, 12, prepare, 0)
    wait_for(stats.at[pl.ds(1, 31)], stat_sem.at[1])
    every = stats[...]
    tops = every[:, 0, :]
    top = jnp.max(tops, axis=0, keepdims=True)
    mass = jnp.sum(every[:, 1, :] * jnp.exp(tops - top), axis=0, keepdims=True)
    got0 = jnp.sum(every[:, 2, :], axis=0, keepdims=True)
    got1 = jnp.sum(every[:, 3, :], axis=0, keepdims=True)
    spread = jnp.log(mass)
    best = jnp.maximum(got0, got1)
    raised0 = jnp.exp(got0 - best)
    raised1 = jnp.exp(got1 - best)
    chosen0 = raised0 / (raised0 + raised1)
    chosen1 = raised1 / (raised0 + raised1)
    rows = jnp.where(which == 0, chosen0, jnp.where(which == 1, chosen1, spread))
    rows = jnp.where(core == 0, rows, pltpu.roll(rows, 64, 1))
    picks[0] = rows
    spread_ref[...] = rows

    def pass_on(w, carry):
        remote(picks.at[0], picks.at[w], pair(pick_sem), jnp.bitwise_xor(dom, 2 * w), tile).start()
        return carry

    lax.fori_loop(1, 4, pass_on, 0, unroll=True)
    lax.fori_loop(THIRD, 15, pack_ship, 0)
    pack(15, 0)
    rb[15, 0] = sb[15, 0]

    for e in range(1, 8):
        t = jnp.bitwise_xor(tile, SHIFT[e])
        remote(sb.at[15, e], rb.at[15, e], (data_send, data_recv.at[15]), jnp.bitwise_xor(dom, e), t).start()
    lax.fori_loop(12, 16, prepare, 0)
    wait_for(picks.at[pl.ds(1, 3)], pick_sem.at[1])
    for w in range(4):
        table[2 * w:2 * w + 2, :] = picks[w, 0:2, :]
    chosen_rows = table[...].astype(BF16)

    def choose(u, carry):
        number = code[u].astype(I32)
        hot = jnp.where(iota((HALF, 256), 0) == (number & 127), 1.0, 0.0).astype(BF16)
        found = jnp.dot(chosen_rows, hot, preferred_element_type=F32)
        keep = iota((8, 256), 0) == ((lane2 >> 6) * 2 + (number >> 7))
        weight[u] = jnp.sum(jnp.where(keep, found, 0.0), axis=0, keepdims=True)
        return carry

    lax.fori_loop(0, 16, choose, 0, unroll=8)

    slab_row = iota((256, 4 * 256), 0).astype(F32).astype(BF16)
    for g in range(4):
        for i in range(4 * g, 4 * g + 4):
            if i == 15:
                wait_for(rb.at[15, pl.ds(1, 7)], data_recv.at[15])
            else:
                wait_for(rb.at[i], data_recv.at[i])
        low_row = jnp.concatenate([low[i] for i in range(4 * g, 4 * g + 4)], axis=1)
        high_row = jnp.concatenate([high[i] for i in range(4 * g, 4 * g + 4)], axis=1)
        share_row = jnp.concatenate([weight[i] for i in range(4 * g, 4 * g + 4)], axis=1)
        if g == 3:
            rows_ref[...] = rb[12:16].reshape(1024, 256)
            power_ref[...] = pm[12:16].reshape(1024, 256)
            label_ref[0:1, :] = low_row
            label_ref[1:2, :] = high_row
            label_ref[2:3, :] = share_row
            break
        low16 = low_row.astype(BF16)

        def insert(b, carry):
            match = slab_row == low16
            rows = rb[4 * g:4 * g + 4].reshape(1024, 256)
            power = pm[4 * g:4 * g + 4].reshape(1024, 256)
            spots = []
            for h in range(2):
                value = jnp.where(high_row == (b + 4 * h).astype(F32), share_row, 0.0).astype(BF16)
                spots.append(jnp.where(match, value, jnp.zeros_like(value)))
            both = jnp.dot(spots[0] + spots[1], power, preferred_element_type=F32)
            for h in range(2):
                at = pl.ds(pl.multiple_of((b + 4 * h) * 256, 256), 256)
                data = jnp.dot(spots[h], rows, preferred_element_type=F32)
                more = both[:, h * HALF:(h + 1) * HALF]
                if g == 0:
                    vol_ref[at, 0:256] = data
                    vol_ref[at, 256:] = more
                else:
                    vol_ref[at, 0:256] += data
                    vol_ref[at, 256:] += more
            return carry

        lax.fori_loop(0, 4, insert, 0)

    wait_for(xw.at[mine], xw_sem.at[0])
    wait_for(meta1.at[pl.ds(1, 15)], m1_sem.at[0])
    wait_for(noise.at[pl.ds(1, 15)], noise_sem.at[0])
    wait_for(info.at[pl.ds(1, 7)], info_sem.at[0])
    wait_for(meta2.at[pl.ds(1, 7)], m2_sem.at[0])
    wait_for(part.at[pl.ds(1, 15)], part_sem.at[0])
    wait_for(stats.at[pl.ds(1, 31)], stat_sem.at[0])
    wait_for(picks.at[pl.ds(1, 3)], pick_sem.at[0])
    wait_for(sb.at[pl.ds(0, 15)], data_send)
    wait_for(sb.at[15, pl.ds(1, 7)], data_send)


def finish(part_ref, rows_ref, power_ref, label_ref, stat_ref, vol_ref, spread_ref):
    b = pl.program_id(0)
    match = iota((256, 1024), 0).astype(F32).astype(BF16) == label_ref[0:1, :].astype(BF16)
    spots = []
    for h in range(2):
        value = jnp.where(label_ref[1:2, :] == (b + 4 * h).astype(F32), label_ref[2:3, :], 0.0).astype(BF16)
        spots.append(jnp.where(match, value, jnp.zeros_like(value)))
    both = jnp.dot(spots[0] + spots[1], power_ref[...], preferred_element_type=F32)
    for h in range(2):
        data = jnp.dot(spots[h], rows_ref[...], preferred_element_type=F32)
        vol_ref[h, :, 0:256] = part_ref[h, :, 0:256] + data
        vol_ref[h, :, 256:] = part_ref[h, :, 256:] + both[:, h * HALF:(h + 1) * HALF]
    spread_ref[...] = stat_ref[2:3, 0:PD]


def shards(images, defocus, noise_weight, references, candidates, route, strips):
    rows = images.reshape(MINE, 2 * HALF)
    focus = defocus[None]
    turned = [jnp.transpose(x[0, 0], (1, 2, 0)) for x in (route, strips)]
    vmem = pl.BlockSpec(memory_space=pltpu.VMEM)
    dma = pltpu.SemaphoreType.DMA
    partial, last_rows, last_power, labels, stat = pl.pallas_call(
        kernel,
        out_shape=(
            jax.ShapeDtypeStruct((STRIPS, WIDE), F32),
            jax.ShapeDtypeStruct((1024, 256), BF16),
            jax.ShapeDtypeStruct((1024, 256), BF16),
            jax.ShapeDtypeStruct((8, 1024), F32),
            jax.ShapeDtypeStruct((8, HALF), F32),
        ),
        in_specs=[vmem, vmem, vmem, vmem, pl.BlockSpec(memory_space=pl.ANY), vmem, vmem],
        out_specs=(vmem,) * 5,
        scratch_shapes=[
            pltpu.VMEM((REFS, ROWS_DEV, 2 * HALF), BF16),
            pltpu.VMEM((CHUNK, DEPTH), BF16),
            pltpu.VMEM((2 * PD, DEPTH), BF16),
            pltpu.VMEM((MINE, 2 * HALF), BF16),
            pltpu.VMEM((MINE, HALF), BF16),
            pltpu.VMEM((2, 16, 8, MINE), F32),
            pltpu.VMEM((2, MINE), F32),
            pltpu.VMEM((2, 32, MINE), BF16),
            pltpu.VMEM((16, 8, 32, 256), BF16),
            pltpu.VMEM((16, 8, 32, 256), BF16),
            pltpu.VMEM((16, 8, 1, HALF), F32),
            pltpu.VMEM((16, 8, 1, HALF), F32),
            pltpu.VMEM((8, 16, 1, HALF), F32),
            pltpu.VMEM((8, MINE), F32),
            pltpu.VMEM((8, 8, HALF), F32),
            pltpu.VMEM((16, 16, HALF), F32),
            pltpu.VMEM((REFS, 2 * PD), F32),
            pltpu.VMEM((16, 64, 2 * PD), F32),
            pltpu.VMEM((32, 8, HALF), F32),
            pltpu.VMEM((4, 8, HALF), F32),
            pltpu.VMEM((16, HALF), F32),
            pltpu.VMEM((8, HALF), F32),
            pltpu.VMEM((16, 1, 256), F32),
            pltpu.VMEM((16, 1, 256), F32),
            pltpu.VMEM((16, 1, 256), F32),
            pltpu.VMEM((16, 1, 256), F32),
            pltpu.VMEM((16, 256, 256), BF16),
            dma((REFS // CHUNK,)),
            dma,
            dma((16,)),
            pltpu.SemaphoreType.REGULAR,
        ] + [dma((2,))] * 8,
        compiler_params=pltpu.CompilerParams(
            collective_id=0, has_side_effects=True, vmem_limit_bytes=56 << 20
        ),
    )(rows, focus, candidates.T, noise_weight, references, *turned)
    half = pl.BlockSpec((2, 256, WIDE), lambda b: (0, b, 0))

    def whole(shape):
        return pl.BlockSpec(shape, lambda b: (0, 0))

    volume, spread = pl.pallas_call(
        finish,
        grid=(4,),
        out_shape=(
            jax.ShapeDtypeStruct((2, STRIPS // 2, WIDE), F32),
            jax.ShapeDtypeStruct((1, PD), F32),
        ),
        in_specs=[half, whole((1024, 256)), whole((1024, 256)), whole((8, 1024)), whole((8, HALF))],
        out_specs=(half, whole((1, PD))),
        compiler_params=pltpu.CompilerParams(vmem_limit_bytes=62 << 20),
    )(partial.reshape(2, STRIPS // 2, WIDE), last_rows, last_power, labels, stat)
    return volume.reshape(STRIPS, WIDE), spread[0]


def solution(mesh):
    in_specs = (
        P("dom", "tile", None),
        P("dom"),
        P("tile", None),
        P(None, "tile", None),
        P("dom", None),
        P("dom", "tile", None, None, None),
        P("dom", "tile", None, None, None),
    )
    out_specs = (P(("dom", "tile"), None), P("dom"))
    return jax.shard_map(shards, mesh=mesh, in_specs=in_specs, out_specs=out_specs, check_vma=False)
```
